32 devices in a mesh: dp: 4 (over z), tensor: 8 (over y, x, core).
Axes of the slice: x: 2, y: 2, z: 4, core: 2. Of those that a mesh axis runs over, the one named last changes fastest.
Arguments:
- hidden_in: bfloat16 [6144, 2048], P(('dp', 'tensor')), may hold values from -6 to 6
- doc_ids: int32 [4, 1536], P('dp'), may hold values from 0 to 11, never falling along the last dimension, each value on 1 to 384 neighbouring positions
- query_weight: bfloat16 [2048, 2048], P(None, 'tensor'), may hold values from -1 to 1
- key_weight: bfloat16 [2048, 2048], P(None, 'tensor'), may hold values from -1 to 1
- value_weight: bfloat16 [2048, 2048], P(None, 'tensor'), may hold values from -0.125 to 0.125
- output_weight: bfloat16 [2048, 2048], P('tensor'), may hold values from -0.125 to 0.125
- gate_weight: bfloat16 [2048, 8192], P(None, 'tensor'), may hold values from -0.125 to 0.125
- up_weight: bfloat16 [2048, 8192], P(None, 'tensor'), may hold values from -0.125 to 0.125
- down_weight: bfloat16 [8192, 2048], P('tensor'), may hold values from -0.0625 to 0.0625
- query_gain: float32 [2048], P('tensor'), may hold values from 0.1 to 1.9
- key_gain: float32 [2048], P('tensor'), may hold values from 0.1 to 1.9
- attention_gain: float32 [2048], replicated, may hold values from 0.5 to 1.5
- feedforward_gain: float32 [2048], replicated, may hold values from 0.5 to 1.5
- out_grad: bfloat16 [6144, 2048], P(('dp', 'tensor')), may hold values from -6 to 6
Outputs:
- result: float32 [6144, 2048], P(('dp', 'tensor'))
- input_grad: float32 [6144, 2048], P(('dp', 'tensor'))
- query_weight_grad: float32 [2048, 2048], P('dp', 'tensor')
- key_weight_grad: float32 [2048, 2048], P('dp', 'tensor')
- value_weight_grad: float32 [2048, 2048], P('dp', 'tensor')
- output_weight_grad: float32 [2048, 2048], P('tensor', 'dp')
- gate_weight_grad: float32 [2048, 8192], P('dp', 'tensor')
- up_weight_grad: float32 [2048, 8192], P('dp', 'tensor')
- down_weight_grad: float32 [8192, 2048], P('tensor', 'dp')
- query_gain_grad: float32 [2048], replicated
- key_gain_grad: float32 [2048], replicated
- attention_gain_grad: float32 [2048], replicated
- feedforward_gain_grad: float32 [2048], replicated
The draws below stay inside these ranges and needn't reach their ends.
All inputs are finite; a program needn't handle non-finite values.
Results may differ from the reference program's by a relative error of at most 0.015.
The reference program's roundings to bfloat16 on the way count: a program that leaves them out, or rounds other values in their place, can miss the bound.
Values may be sent and summed in bfloat16 or wider, within the bound.
No kernel may reach another device: no remote copies, remote signals or barrier semaphores. Data moves between devices by JAX's collectives and lax.ppermute only.
A program may use at most 256 MiB of HBM per device.

```python
import math
import jax
import jax.numpy as jnp
import numpy as np
from jax import lax

D = 2048
HEADS = 16
HEAD_DIM = 128
FF = 8192
DOCS = 12
LENGTH = 1536
DOC_MOST = 384
TOKENS = 6144
N_DP = 4


def ramped_columns(key, ramp_base):
    entry_key, scale_key = jax.random.split(key)
    entries = jnp.clip(jax.random.normal(entry_key, (D, D), jnp.float32), -6.0, 6.0)
    head_place = (jnp.arange(D) // HEAD_DIM).astype(jnp.float32)
    ramp = jnp.exp(jnp.log(ramp_base) * head_place / max(HEADS - 1, 1))
    jitter = jnp.exp(jax.random.uniform(scale_key, (D,), jnp.float32, -0.35, 0.35))
    scaled = entries * (ramp * jitter)[None, :] * D ** (-0.5)
    return jnp.clip(scaled, -1.0, 1.0).astype(jnp.bfloat16)


def draw_query_weight(key, part):
    key = jax.random.fold_in(key, 11)
    ramp_base = 3.0
    return ramped_columns(key, ramp_base)


def draw_key_weight(key, part):
    key = jax.random.fold_in(key, 23)
    ramp_base = 3.0
    return ramped_columns(key, ramp_base)


def shard_levels(own_key, extent, cuts, smallest, top_value):
    level, own = 1.0, jax.random.fold_in(own_key, 6)
    for axis_at, blocks in cuts:
        heights = jnp.exp(jax.random.uniform(jax.random.fold_in(own, axis_at), (blocks,), jnp.float32, smallest / len(cuts), top_value / len(cuts)))
        level = level * jnp.repeat(heights, extent[axis_at] // blocks).reshape([-1 if axis == axis_at else 1 for axis in range(len(extent))])
    return level


def split_up(amount, total, bound, slope):
    portions = [(1 << 20) // math.isqrt(standing ** slope) + 1 for standing in range(2, amount + 1)]
    rest, counts = total - bound - (amount - 1), [1] * (amount - 1)
    while rest > 0:
        candidates = [i for i in range(amount - 1) if counts[i] < bound]
        mass, left = sum([portions[i] for i in candidates]), rest
        for i in candidates:
            addition = min(bound - counts[i], max(1, left * portions[i] // mass), rest)
            counts[i] = counts[i] + addition
            rest = rest - addition
    return np.array([bound] + counts)


def uneven_parts(key, number_of, total, limit, skew):
    if number_of == 2:
        one = jax.random.randint(key, (), max(1, total - limit), min(limit, total - 1) + 1)
        return jnp.stack([one, total - one])
    sizes = jnp.asarray(split_up(number_of, total, limit, skew), jnp.int32)
    twos = (number_of - 1) // 2
    source_of, sink = sizes[1:1 + 2 * twos:2], sizes[2:2 + 2 * twos:2]
    slack = jnp.minimum(source_of - 1, limit - sink)
    moved = jax.random.randint(jax.random.fold_in(key, 1), (twos,), 0, 1 << 20) % (slack + 1)
    sizes = sizes.at[1:1 + 2 * twos:2].set(source_of - moved).at[2:2 + 2 * twos:2].set(sink + moved)
    return sizes[jax.random.permutation(jax.random.fold_in(key, 2), number_of)]


def centred(key, shape, width, reach, cuts=(), kind=jnp.bfloat16):
    factor_of = shard_levels(key, shape, cuts, -0.22, 0.18) if cuts else 1.0
    values = jax.random.normal(key, shape, jnp.float32) * width * factor_of
    return jnp.minimum(jnp.maximum(values, -reach), reach).astype(kind)


def setup_inputs(seed: int = 0) -> dict:
    key_of = jax.random.split(jax.random.key(seed), 15)
    hidden_in = centred(key_of[0], (TOKENS, D), 1.0, 6.0, ((0, 32),))
    doc_ids = jax.vmap(lambda own: jnp.searchsorted(jnp.cumsum(uneven_parts(own, DOCS, LENGTH, DOC_MOST, 1)), jnp.arange(LENGTH), side="right"))(jax.random.split(key_of[1], N_DP)).reshape((N_DP, LENGTH)).astype(jnp.int32)
    query_weight = draw_query_weight(jax.random.fold_in(key_of[14], 71), 0)
    key_weight = draw_key_weight(jax.random.fold_in(key_of[14], 71), 0)
    value_weight = centred(key_of[4], (D, D), D ** -0.5, 0.125, ((1, 8),))
    output_weight = centred(key_of[5], (D, D), D ** -0.5, 0.125, ((0, 8),))
    gate_weight = centred(key_of[6], (D, FF), D ** -0.5, 0.125, ((1, 8),))
    up_weight = centred(key_of[7], (D, FF), D ** -0.5, 0.125, ((1, 8),))
    down_weight = centred(key_of[8], (FF, D), FF ** -0.5, 0.0625, ((0, 8),))
    query_gain = jnp.clip(1.0 + 0.18 * jax.random.normal(key_of[9], (D,), jnp.float32), 0.1, 1.9)
    key_gain = jnp.clip(1.0 + 0.18 * jax.random.normal(key_of[10], (D,), jnp.float32), 0.1, 1.9)
    attention_gain = jnp.clip(1.0 + 0.1 * jax.random.normal(key_of[11], (D,), jnp.float32), 0.5, 1.5)
    feedforward_gain = jnp.clip(1.0 + 0.1 * jax.random.normal(key_of[12], (D,), jnp.float32), 0.5, 1.5)
    out_grad = centred(key_of[13], (TOKENS, D), 1.0, 6.0, ((0, 32),))
    return {"hidden_in": hidden_in, "doc_ids": doc_ids, "query_weight": query_weight, "key_weight": key_weight, "value_weight": value_weight, "output_weight": output_weight, "gate_weight": gate_weight, "up_weight": up_weight, "down_weight": down_weight, "query_gain": query_gain, "key_gain": key_gain, "attention_gain": attention_gain, "feedforward_gain": feedforward_gain, "out_grad": out_grad}


norm_eps = 1e-06
rope_base = 500000.0
highest = lax.Precision.HIGHEST

@jax.custom_vjp
def low(v):
    return lax.optimization_barrier(v.astype(jnp.bfloat16)).astype(jnp.float32)

@jax.custom_vjp
def low_back(v):
    return v

def low_keep(v):
    return (low(v), None)

def low_pass(kept, grad):
    return (grad,)

def back_keep(v):
    return (v, None)

def back_low(kept, grad):
    return (low(grad),)
low.defvjp(low_keep, low_pass)
low_back.defvjp(back_keep, back_low)

def matmul(left, right):
    return jnp.dot(left, right, precision=highest, preferred_element_type=jnp.float32)

def rope_tables(length, head_dim):
    half = head_dim // 2
    freq = rope_base ** (-(2.0 * jnp.arange(half, dtype=jnp.float32)) / head_dim)
    angle = jnp.arange(length, dtype=jnp.float32)[:, None] * freq[None, :]
    cosine = jnp.concatenate([jnp.cos(angle), jnp.cos(angle)], axis=1)
    sine = jnp.concatenate([jnp.sin(angle), jnp.sin(angle)], axis=1)
    return (cosine[:, None, :], sine[:, None, :])

def rotate(value, cosine, sine):
    half = value.shape[-1] // 2
    turned = jnp.concatenate([-value[..., half:], value[..., :half]], axis=-1)
    return value * cosine + turned * sine

def normalize(value, gain):
    return value * lax.rsqrt(lax.optimization_barrier(jnp.mean(value * value, axis=-1, keepdims=True)) + norm_eps) * gain

def attention(query, key, value, documents):
    length = query.shape[0]
    span = min(512, length)
    count = length // span
    scale = HEAD_DIM ** (-0.5)
    columns = jnp.arange(length)

    def one_block(inputs):
        query_block, rows, doc_block = inputs
        scores = jnp.einsum('bhd,lhd->hbl', query_block, key, precision=highest) * scale
        scores = low_back(scores)
        allowed = (columns[None, :] <= rows[:, None]) & (documents[None, :] == doc_block[:, None])
        scores = jnp.where(allowed[None], scores, -1e+30)
        top = lax.optimization_barrier(jnp.max(scores, axis=-1, keepdims=True))
        weights = jnp.exp(scores - top)
        shares = low(weights / lax.optimization_barrier(jnp.sum(weights, axis=-1, keepdims=True)))
        return jnp.einsum('hbl,lhd->bhd', shares, value, precision=highest)
    blocks = lax.map(jax.checkpoint(one_block), (query.reshape(count, span, HEADS, HEAD_DIM), jnp.arange(length).reshape(count, span), documents.reshape(count, span)))
    return blocks.reshape(length, HEADS * HEAD_DIM)

def block_forward(hidden, query_weight, key_weight, value_weight, output_weight, gate_weight, up_weight, down_weight, query_gain, key_gain, attention_gain, feedforward_gain, documents, cosine, sine):
    length = hidden.shape[0]
    query_raw = low_back(matmul(hidden, query_weight))
    key_raw = low_back(matmul(hidden, key_weight))
    value = low(low_back(matmul(hidden, value_weight)))
    query = low(rotate(normalize(query_raw, query_gain).reshape(length, HEADS, HEAD_DIM), cosine, sine))
    key = low(rotate(normalize(key_raw, key_gain).reshape(length, HEADS, HEAD_DIM), cosine, sine))
    attended = low(low_back(attention(query, key, value.reshape(length, HEADS, HEAD_DIM), documents)))
    middle = hidden + normalize(low_back(matmul(attended, output_weight)), attention_gain)
    middle_low = low(middle)
    gate = low_back(matmul(middle_low, gate_weight))
    up = low_back(matmul(middle_low, up_weight))
    activated = low(jax.nn.silu(gate) * up)
    return middle + normalize(low_back(matmul(activated, down_weight)), feedforward_gain)

def reference(hidden_in, doc_ids, query_weight, key_weight, value_weight, output_weight, gate_weight, up_weight, down_weight, query_gain, key_gain, attention_gain, feedforward_gain, out_grad):
    weights = tuple((array.astype(jnp.float32) for array in (query_weight, key_weight, value_weight, output_weight, gate_weight, up_weight, down_weight, query_gain, key_gain, attention_gain, feedforward_gain)))
    cosine, sine = rope_tables(LENGTH, HEAD_DIM)
    rows_in = hidden_in.astype(jnp.float32).reshape(N_DP, LENGTH, D)
    grads_in = out_grad.astype(jnp.float32).reshape(N_DP, LENGTH, D)

    def one_row(carry, inputs):
        hidden, documents, grad = inputs

        def forward(hidden, *parameters):
            return block_forward(hidden, *parameters, documents, cosine, sine)
        output, backward = jax.vjp(forward, hidden, *weights)
        cotangents = backward(grad)
        summed = tuple((first + second for first, second in zip(carry, cotangents[1:])))
        return (summed, (output, cotangents[0]))
    initial = tuple((jnp.zeros_like(array) for array in weights))
    totals, (outputs, input_grads) = lax.scan(one_row, initial, (rows_in, doc_ids, grads_in))
    return (outputs.reshape(TOKENS, D), input_grads.reshape(TOKENS, D), totals[0], totals[1], totals[2], totals[3], totals[4], totals[5], totals[6], totals[7], totals[8], totals[9], totals[10])
```

```python
import functools

import jax
import jax.numpy as jnp
from jax import lax
from jax.experimental import pallas as pl
from jax.experimental.pallas import tpu as pltpu
from jax.sharding import PartitionSpec as P

HEAD_DIM = 128
BF16 = jnp.bfloat16
F32 = jnp.float32

norm_eps = 1e-06
rope_base = 500000.0


def contract_rows(left, right):
    return lax.dot_general(left, right, (((0,), (0,)), ((), ())), preferred_element_type=F32)


def times_transposed(left, right):
    return lax.dot_general(left, right, (((1,), (1,)), ((), ())), preferred_element_type=F32)


def times(left, right):
    return jnp.dot(left, right, preferred_element_type=F32)


def rope_tables(length, head_dim):
    half = head_dim // 2
    freq = rope_base ** (-(2.0 * jnp.arange(half, dtype=F32)) / head_dim)
    angle = jnp.arange(length, dtype=F32)[:, None] * freq[None, :]
    cosine, sine = jnp.cos(angle), jnp.sin(angle)
    return (
        jnp.concatenate([cosine, cosine], axis=1),
        jnp.concatenate([-sine, sine], axis=1),
    )


def norm_back(grad, unit, inverse, gain):
    inner = grad * gain
    return inverse * (inner - unit * jnp.mean(inner * unit, axis=1, keepdims=True))


class PairedCores:
    def __init__(self):
        turn = lambda low, high: [(i, i ^ (low if i % 2 == 0 else high)) for i in range(8)]
        self.first, self.second, self.core = turn(2, 4), turn(4, 2), turn(1, 1)

    def send(self, value, way):
        return lax.ppermute(value, "tensor", way)

    def order(self):
        me = lax.axis_index("tensor")
        near = jnp.where(me % 2 == 0, 2, 4)
        far = 6 - near
        return jnp.stack([me ^ near, me ^ far, me, me ^ 6, me ^ 1 ^ far, me ^ 1 ^ near, me ^ 1, me ^ 7])

    def gather(self, own, meanwhile=None, early=None):
        first, second = self.send(own, self.first), self.send(own, self.second)
        other = self.send(own, self.core)
        if meanwhile is not None:
            second, meanwhile = lax.optimization_barrier((second, meanwhile))
        opposite = self.send(second, self.first)
        first_other, second_other = self.send(first, self.core), self.send(second, self.core)
        groups = [[own, other], [first, second, first_other, second_other]]
        made = None
        if early is not None:
            opposite, made = lax.optimization_barrier((opposite, early(*groups)))
        groups.append([opposite, self.send(opposite, self.core)])
        return groups, meanwhile, made

    def whole(self, groups):
        near, middle, last = groups
        if not isinstance(near, list):
            near, middle, last = jnp.split(near, 2), jnp.split(middle, 4), jnp.split(last, 2)
        first, second, first_other, second_other = middle
        return [first, second, near[0], last[0], first_other, second_other, near[1], last[1]]

    def groups(self, whole):
        first, second, own, opposite, first_other, second_other, other, opposite_other = jnp.split(whole, 8)
        groups = [[own, other], [first, second, first_other, second_other], [opposite, opposite_other]]
        return [jnp.concatenate(group, axis=0) for group in groups]

    def scatter(self, halves, product, meanwhile=None, late=None):
        mine, others = halves
        from_core = self.send(product(others).astype(BF16), self.core)
        total = product(mine) + from_core.astype(F32)
        first, second, own, opposite = jnp.split(total, 4)
        sent = opposite.astype(BF16), first.astype(BF16)
        passing, from_first = (self.send(part, self.first) for part in sent)
        if meanwhile is not None:
            passing, meanwhile = lax.optimization_barrier((passing, meanwhile(sent)))
        from_second = self.send((second + passing.astype(F32)).astype(BF16), self.second)
        if late is not None:
            from_second, late = lax.optimization_barrier((from_second, late(passing)))
        return own + from_first.astype(F32) + from_second.astype(F32), meanwhile, late

    def add(self, value):
        for bit in (1, 2, 4):
            value = value + self.send(value, [(i, i ^ bit) for i in range(8)])
        return value


class AnyDevices:
    def __init__(self, size):
        self.size = size

    def order(self):
        return jnp.arange(self.size)

    def gather(self, own, meanwhile=None, early=None):
        return [[lax.all_gather(own, "tensor", axis=0, tiled=True)]], meanwhile, []

    def groups(self, whole):
        return [whole]

    def whole(self, groups):
        return groups[0] if isinstance(groups[0], list) else groups

    def scatter(self, halves, product, meanwhile=None, late=None):
        part = product(jnp.concatenate(halves, axis=0)).astype(BF16)
        total = lax.psum_scatter(part, "tensor", scatter_dimension=0, tiled=True).astype(F32)
        return total, meanwhile, late

    def add(self, value):
        return lax.psum(value, "tensor")


def in_pairs(step):
    return [(i, i ^ step) for i in range(4)]


def scatter_rows(part, dimension):
    return lax.psum_scatter(part, "dp", scatter_dimension=dimension, tiled=True).astype(F32)


def from_neighbour(part):
    both = lax.all_gather(part, "dp", axis_index_groups=[[0, 1], [2, 3]])
    return lax.dynamic_index_in_dim(both, 1 - lax.axis_index("dp") % 2, 0, keepdims=False)


def piece_of(part, dimension, place):
    size = part.shape[dimension] // 4
    return lax.dynamic_slice_in_dim(part, place * size, size, dimension)


def add_rows(value, count):
    if count != 4:
        return lax.psum(value, "dp")
    one, two, three = (lax.ppermute(value, "dp", in_pairs(step)) for step in (1, 2, 3))
    return value + one, two, three


def turned(value):
    return pltpu.roll(value, HEAD_DIM // 2, 1)


def scale_of(sums, at, width):
    return lax.rsqrt(sums[:, at : at + 1] * (1.0 / width) + norm_eps)


def allowed_in(docs_col, docs_row, block, back):
    window = (back + 1) * block
    rows = lax.broadcasted_iota(jnp.int32, (block, window), 0)
    columns = lax.broadcasted_iota(jnp.int32, (block, window), 1)
    return (docs_col == docs_row) & (columns <= rows + back * block)


def places_of(b, block, back):
    start = pl.multiple_of(b * block, block)
    return pl.ds(start, block), pl.ds(start + back * block, block), pl.ds(start, (back + 1) * block)


def attend_kernel(
    shape, order, raw, sums, gains, cosine, sine, docs_col, docs_row, attended, query, key, value, logsum
):
    blocks, block, width, local, back, scale = shape
    heads = local // HEAD_DIM
    for ref in (key, value):
        ref[: back * block, :] = jnp.zeros((back * block, local), BF16)

    def step(b, carry):
        at = order[b]
        rows, later, window = places_of(b, block, back)
        total = sums[b]
        cos, sin = cosine[rows, :], sine[rows, :]
        for which in range(2):
            inverse = scale_of(total, which, width)
            for h in range(heads):
                lanes = slice(h * HEAD_DIM, (h + 1) * HEAD_DIM)
                own = slice(which * local + h * HEAD_DIM, which * local + (h + 1) * HEAD_DIM)
                v = raw[at, :, own] * inverse * gains[which : which + 1, lanes]
                v = (v * cos + turned(v) * sin).astype(BF16)
                if which == 0:
                    query[rows, lanes] = v
                else:
                    key[later, lanes] = v
        value[later, :] = raw[at, :, 2 * local :].astype(BF16)
        allowed = allowed_in(docs_col[rows, :], docs_row[b], block, back)
        for h in range(heads):
            lanes = slice(h * HEAD_DIM, (h + 1) * HEAD_DIM)
            scores = times_transposed(query[rows, lanes], key[window, lanes]) * scale
            scores = jnp.where(allowed, scores, -1e30)
            top = jnp.max(scores, axis=1, keepdims=True)
            weights = jnp.exp(scores - top)
            mass = jnp.sum(weights, axis=1, keepdims=True)
            shares = (weights * (1.0 / mass)).astype(BF16)
            attended[at, :, lanes] = times(shares, value[window, lanes]).astype(BF16)
            logsum[h, rows, :] = top + jnp.log(mass)
        return carry

    lax.fori_loop(0, blocks, step, 0)


def attend_back_kernel(
    shape,
    order,
    raw,
    sums,
    gains,
    cosine,
    sine,
    docs_col,
    docs_row,
    query,
    key,
    value,
    logsum,
    grad,
    inner,
    grad_value,
    products,
    gain_parts,
    grad_query_sum,
    grad_key_sum,
    grad_value_sum,
):
    blocks, block, width, local, back, scale = shape
    heads = local // HEAD_DIM
    grad_key_sum[...] = jnp.zeros(grad_key_sum.shape, F32)
    grad_value_sum[...] = jnp.zeros(grad_value_sum.shape, F32)
    gain_parts[...] = jnp.zeros(gain_parts.shape, F32)

    def step(b, carry):
        at = order[b]
        rows, later, window = places_of(b, block, back)
        allowed = allowed_in(docs_col[rows, :], docs_row[b], block, back)
        for h in range(heads):
            lanes = slice(h * HEAD_DIM, (h + 1) * HEAD_DIM)
            q, k, v, g = query[rows, lanes], key[window, lanes], value[window, lanes], grad[at, :, lanes]
            scores = times_transposed(q, k) * scale
            chances = jnp.exp(jnp.where(allowed, scores, -1e30) - logsum[h, rows, :])
            grad_shares = times_transposed(g, v)
            offset = jnp.sum(chances * grad_shares, axis=1, keepdims=True)
            grad_scores = (chances * (grad_shares - offset)).astype(BF16)
            grad_query_sum[rows, lanes] = times(grad_scores, k) * scale
            grad_key_sum[window, lanes] += contract_rows(grad_scores, q) * scale
            grad_value_sum[window, lanes] += contract_rows(chances.astype(BF16), g)
        return carry

    lax.fori_loop(0, blocks, step, 0)

    def finish(b, carry):
        at = order[b]
        rows, later, window = places_of(b, block, back)
        total = sums[b]
        cos, sin = cosine[rows, :], sine[rows, :]
        grad_value[at] = grad_value_sum[later, :].astype(BF16)
        for which in range(2):
            inverse = scale_of(total, which, width)
            dots = jnp.zeros((8, block), F32)
            ones = jnp.ones((8, HEAD_DIM), F32)
            for h in range(heads):
                lanes = slice(h * HEAD_DIM, (h + 1) * HEAD_DIM)
                own = slice(which * local + h * HEAD_DIM, which * local + (h + 1) * HEAD_DIM)
                unit = raw[at, :, own] * inverse
                g = grad_query_sum[rows, lanes] if which == 0 else grad_key_sum[later, lanes]
                g = g * cos + turned(g * sin)
                gain_parts[which : which + 1, lanes] += jnp.sum(g * unit, axis=0, keepdims=True)
                c = g * gains[which : which + 1, lanes]
                inner[at, :, own] = c
                dots = dots + lax.dot_general(
                    ones, c * unit, (((1,), (1,)), ((), ())), precision=lax.Precision.HIGHEST,
                    preferred_element_type=F32,
                )
            products[b, which : which + 1, :] = dots[:1]
        return carry

    lax.fori_loop(0, blocks, finish, 0)


def whole_specs(count):
    return [pl.BlockSpec(memory_space=pltpu.SMEM)] + [pl.BlockSpec(memory_space=pltpu.VMEM)] * count


def attend(shape, order, raw, sums, gains, cosine, sine, docs_col, docs_row):
    blocks, block, width, local, back, scale = shape
    heads, length = local // HEAD_DIM, blocks * block
    padded = length + back * block
    return pl.pallas_call(
        functools.partial(attend_kernel, shape),
        out_shape=(
            jax.ShapeDtypeStruct((blocks, block, local), BF16),
            jax.ShapeDtypeStruct((length, local), BF16),
            jax.ShapeDtypeStruct((padded, local), BF16),
            jax.ShapeDtypeStruct((padded, local), BF16),
            jax.ShapeDtypeStruct((heads, length, 1), F32),
        ),
        in_specs=whole_specs(7),
        out_specs=(pl.BlockSpec(memory_space=pltpu.VMEM),) * 5,
        compiler_params=pltpu.CompilerParams(vmem_limit_bytes=24 * 2**20),
        cost_estimate=pl.CostEstimate(flops=4 * 10**9, bytes_accessed=10**7, transcendentals=2 * 10**6),
    )(order, raw, sums, gains, cosine, sine, docs_col, docs_row)


def attend_back(shape, order, raw, sums, gains, cosine, sine, docs_col, docs_row, query, key, value, logsum, grad):
    blocks, block, width, local, back, scale = shape
    length = blocks * block
    padded = length + back * block
    return pl.pallas_call(
        functools.partial(attend_back_kernel, shape),
        out_shape=(
            jax.ShapeDtypeStruct((blocks, block, 2 * local), F32),
            jax.ShapeDtypeStruct((blocks, block, local), BF16),
            jax.ShapeDtypeStruct((blocks, 2, block), F32),
            jax.ShapeDtypeStruct((2, local), F32),
        ),
        in_specs=whole_specs(12),
        out_specs=(pl.BlockSpec(memory_space=pltpu.VMEM),) * 4,
        scratch_shapes=[
            pltpu.VMEM((length, local), F32),
            pltpu.VMEM((padded, local), F32),
            pltpu.VMEM((padded, local), F32),
        ],
        compiler_params=pltpu.CompilerParams(vmem_limit_bytes=36 * 2**20),
        cost_estimate=pl.CostEstimate(flops=8 * 10**9, bytes_accessed=2 * 10**7, transcendentals=2 * 10**6),
    )(order, raw, sums, gains, cosine, sine, docs_col, docs_row, query, key, value, logsum, grad)


TILE = 256


def gated_grad(grad_act, gate, up):
    sigma = jax.nn.sigmoid(gate)
    grad_gate = grad_act * up * sigma * (1.0 + gate * (1.0 - sigma))
    return grad_gate.astype(BF16), (grad_act * gate * sigma).astype(BF16)


def feed_back_kernel(count, *refs):
    grads, (weight, gate, up) = refs[:count], refs[count : count + 3]
    *_, mine, others, rows = refs
    block, tile = grads[0].shape[0], weight.shape[0]
    units, half = mine.shape[-1] // 2, rows.shape[0] // 2
    j = pl.program_id(0)

    @pl.when(j == 0)
    def _():
        for at, grad in enumerate(grads):
            rows[at * block : (at + 1) * block, :] = grad[...]

    grad_act = times_transposed(rows[...], weight[...])
    start = pl.multiple_of(j * tile, tile)
    for at, part in zip((start, start + units), gated_grad(grad_act, gate[...], up[...])):
        for out, own in ((mine, part[:half]), (others, part[half:])):
            out[:, :, pl.ds(at, tile)] = own.reshape(out.shape[:2] + (tile,))


def feed_back(grads, down_weight, both, slot, slots, before=()):
    count, width = len(grads), grads[0].shape[1]
    units, tile = down_weight.shape[0], min(TILE, down_weight.shape[0])
    tiles, rows = units // tile, sum(grad.shape[0] for grad in grads)
    in_specs = [pl.BlockSpec(grad.shape, lambda j: (0, 0)) for grad in grads] + [
        pl.BlockSpec((tile, width), lambda j: (j, 0)),
        pl.BlockSpec((rows, tile), lambda j: (0, j)),
        pl.BlockSpec((rows, tile), lambda j: (0, j + tiles)),
    ]
    in_specs += [pl.BlockSpec(memory_space=pl.ANY)] * len(before)
    args = [*grads, down_weight, both, both, *before]
    part = rows // (2 * slots)
    return pl.pallas_call(
        functools.partial(feed_back_kernel, count),
        grid=(tiles,),
        out_shape=(jax.ShapeDtypeStruct((4, part, 2 * units), BF16),) * 2,
        in_specs=in_specs,
        out_specs=(pl.BlockSpec((slots, part, 2 * units), lambda j: (slot // slots, 0, 0)),) * 2,
        scratch_shapes=[pltpu.VMEM((rows, width), BF16)],
        input_output_aliases={count + 3 + at: at for at in range(len(before))},
        compiler_params=pltpu.CompilerParams(vmem_limit_bytes=(8 + 7 * rows // 192) * 2**20),
        cost_estimate=pl.CostEstimate(
            flops=2 * rows * width * units,
            bytes_accessed=2 * units * width + 12 * rows * units + 2 * rows * width,
            transcendentals=rows * units,
        ),
    )(*args)


def pieces_kernel(plan, count, place, *refs):
    sources, outs, sems = refs[:count], refs[count:-1], refs[-1]
    copies = []
    for out, parts in zip(outs, plan):
        size = out.shape[1]
        columns = pl.ds(pl.multiple_of(place[0] * size, size), size)
        at = 0
        for source, start, rows in parts:
            copies.append(
                pltpu.make_async_copy(
                    sources[source].at[pl.ds(start, rows), columns],
                    out.at[pl.ds(at, rows), :],
                    sems.at[len(copies)],
                )
            )
            at += rows
    for copy in copies:
        copy.start()
    for copy in copies:
        copy.wait()


def pieces_of(sources, plan, place, count=4):
    size = sources[0].shape[1] // count
    shapes = [(sum(rows for _, _, rows in parts), size) for parts in plan]
    return pl.pallas_call(
        functools.partial(pieces_kernel, plan, len(sources)),
        out_shape=[jax.ShapeDtypeStruct(shape, BF16) for shape in shapes],
        in_specs=[pl.BlockSpec(memory_space=pltpu.SMEM)] + [pl.BlockSpec(memory_space=pltpu.HBM)] * len(sources),
        out_specs=[pl.BlockSpec(memory_space=pltpu.HBM)] * len(plan),
        scratch_shapes=[pltpu.SemaphoreType.DMA((sum(len(parts) for parts in plan),))],
        compiler_params=pltpu.CompilerParams(vmem_limit_bytes=2**20),
        cost_estimate=pl.CostEstimate(
            flops=0, bytes_accessed=sum(4 * rows * columns for rows, columns in shapes), transcendentals=0
        ),
    )(jnp.reshape(place, (1,)).astype(jnp.int32), *sources)


def joined_rows(blocks):
    return pieces_of(blocks, [[(at, 0, block.shape[0]) for at, block in enumerate(blocks)]], 0, 1)[0]


def body(
    sizes,
    hidden_in,
    doc_ids,
    query_weight,
    key_weight,
    value_weight,
    output_weight,
    gate_weight,
    up_weight,
    down_weight,
    query_gain,
    key_gain,
    attention_gain,
    feedforward_gain,
    out_grad,
):
    tensor, rows = sizes["tensor"], sizes["dp"]
    moves = PairedCores() if tensor == 8 else AnyDevices(tensor)
    width = hidden_in.shape[1]
    local = query_weight.shape[1]
    hidden_units = gate_weight.shape[1]
    documents = doc_ids[0]
    length = documents.shape[0]
    block = length // tensor
    most = length // 4
    back = -(-(most - 1) // block)
    shape = (tensor, block, width, local, back, HEAD_DIM ** (-0.5))

    places = moves.order()
    steps = jnp.arange(tensor, dtype=jnp.int32)
    meets = places[None, :] == steps[:, None]
    order = jnp.sum(jnp.where(meets, steps[None, :], 0), axis=1)

    def in_row(value):
        parts = value.reshape(2, 1, tensor, block)
        return jnp.sum(jnp.where(meets[None, :, :, None], parts, 0.0), axis=2).reshape(2, length)

    def as_arrived(value):
        parts = value.reshape(2, tensor, 1, block)
        return jnp.sum(jnp.where(meets[None, :, :, None], parts, 0.0), axis=1).reshape(2, length)

    cosine, sine = rope_tables(length, HEAD_DIM)
    docs_col = documents[:, None]
    padded = jnp.concatenate([jnp.full((back * block,), -1, jnp.int32), documents])
    docs_row = jnp.stack([padded[b * block : (b + back + 1) * block] for b in range(tensor)])[:, None, :]
    gains = jnp.stack([query_gain, key_gain])

    def row_of(groups):
        return jnp.concatenate(moves.whole(groups), axis=0)

    def joined(group):
        return jnp.concatenate(group, axis=0)

    weight_qkv = jnp.concatenate([query_weight, key_weight, value_weight], axis=1)
    weight_gate_up = jnp.concatenate([gate_weight, up_weight], axis=1)
    paired = rows == 4 and tensor == 8

    def halves_of(whole):
        return jnp.split(whole, 2)

    def raw_of(*groups):
        return [times(joined(group), weight_qkv) for group in groups]

    hidden_groups, _, raw = moves.gather(hidden_in, early=raw_of)
    raw = row_of(raw + raw_of(hidden_groups[-1]))
    squares = jnp.stack(
        [
            jnp.sum(jnp.square(raw[:, :local]), axis=1),
            jnp.sum(jnp.square(raw[:, local : 2 * local]), axis=1),
        ]
    )
    sums = moves.add(in_row(squares))
    raw_blocks = raw.reshape(tensor, block, 3 * local)
    tables = (order, raw_blocks, sums.T.reshape(tensor, block, 2), gains, cosine, sine, docs_col, docs_row)
    attended_blocks, query, key, value, logsum = attend(shape, *tables)
    attended = attended_blocks.reshape(length, local)
    attn_proj, _, _ = moves.scatter(halves_of(attended), lambda part: times(part, output_weight))
    attn_scale = lax.rsqrt(jnp.mean(attn_proj * attn_proj, axis=1, keepdims=True) + norm_eps)
    attn_unit = attn_proj * attn_scale
    middle = hidden_in.astype(F32) + attn_unit * attention_gain
    middle_low = middle.astype(BF16)

    def activate(both):
        gate, up = both[:, :hidden_units], both[:, hidden_units:]
        return (gate * jax.nn.sigmoid(gate) * up).astype(BF16)

    def both_of(*groups):
        both = [times(joined(group), weight_gate_up) for group in groups]
        return both, [activate(part) for part in both]

    def to_pair(value):
        return lax.ppermute(value, "dp", in_pairs(2))

    hidden_all = joined_rows(moves.whole(hidden_groups)) if tensor == 8 else hidden_groups[0][0]
    middle_groups, hidden_all, made = moves.gather(middle_low, hidden_all, both_of)
    if paired:
        middle_groups[-1], pair_middle = lax.optimization_barrier((middle_groups[-1], to_pair(middle_low)))
        pair_middle_all = lax.all_gather(pair_middle, "tensor", axis=0, tiled=True)
    both_groups, activated = (early + late for early, late in zip(made or ([], []), both_of(middle_groups[-1])))
    activated = row_of(activated)
    mlp_proj, _, _ = moves.scatter(halves_of(activated), lambda part: times(part, down_weight))
    mlp_scale = lax.rsqrt(jnp.mean(mlp_proj * mlp_proj, axis=1, keepdims=True) + norm_eps)
    mlp_unit = mlp_proj * mlp_scale
    result = middle + mlp_unit * feedforward_gain

    grad_out = out_grad.astype(F32)
    grad_mlp = norm_back(grad_out, mlp_unit, mlp_scale, feedforward_gain).astype(BF16)
    feedforward_part = jnp.sum(grad_out * mlp_unit, axis=0)
    pair_both = None
    if paired:
        pair_middle_all, grad_mlp = lax.optimization_barrier((pair_middle_all, grad_mlp))
        pair_both = times(pair_middle_all, weight_gate_up)

    def back_early(near, beside):
        part = feed_back(near, down_weight, both_groups[0], 2, 1)
        part = feed_back(beside, down_weight, both_groups[1], 0, 2, part)
        return part, to_pair(grad_mlp) if paired else None

    grad_mlp_groups, pair_both, made = moves.gather(grad_mlp, pair_both, back_early)
    if tensor == 8:
        made, pair_grad_mlp = made
        grad_gate_up = feed_back(grad_mlp_groups[-1], down_weight, both_groups[2], 3, 1, made)
        grad_gate_up = [half.reshape(length // 2, 2 * hidden_units) for half in grad_gate_up]
    else:
        grad_act = times_transposed(grad_mlp_groups[0][0], down_weight)
        both = both_groups[0]
        grad_gate_up = gated_grad(grad_act, both[:, :hidden_units], both[:, hidden_units:])
        grad_gate_up = halves_of(jnp.concatenate(grad_gate_up, axis=1))
    if paired:
        grad_gate_up, pair_activated = lax.optimization_barrier((grad_gate_up, activate(pair_both)))
        pair_grad_mlp_all = lax.all_gather(pair_grad_mlp, "tensor", axis=0, tiled=True)

    me = lax.axis_index("dp")
    half_rows = length // 2

    def own_weight_pieces(place):
        blocks = moves.whole(middle_groups) + moves.whole(grad_mlp_groups)
        part = [(at, 0, block) for at in range(16)]
        mine, others, grads = pieces_of(blocks, [part[:4], part[4:8], part[8:]], place)
        return [
            contract_rows(activated, grads),
            contract_rows(mine, grad_gate_up[0]) + contract_rows(others, grad_gate_up[1]),
        ]

    def pair_weight_pieces(place):
        plan = [[(0, 0, half_rows)], [(0, half_rows, half_rows)], [(1, 0, length)]]
        first, second, grads = pieces_of([pair_middle_all, pair_grad_mlp_all], plan, place)
        return [
            contract_rows(pair_activated, grads),
            contract_rows(first, pair_gate_up[0]) + contract_rows(second, pair_gate_up[1]),
        ]

    def own_away(sent):
        nonlocal grad_mlp_groups, middle_groups
        grad_mlp_groups, middle_groups, _ = lax.optimization_barrier((grad_mlp_groups, middle_groups, sent))
        return own_weight_pieces(me ^ 1)

    def pair_back(passing):
        grads, _ = lax.optimization_barrier((pair_grad_mlp_all, passing))
        pair_gate_up = feed_back([grads], down_weight, pair_both, 0, 4)
        return [half.reshape(half_rows, 2 * hidden_units) for half in pair_gate_up]

    back_part, away, pair_gate_up = moves.scatter(
        grad_gate_up,
        lambda part: times_transposed(part, weight_gate_up),
        own_away if paired else None,
        pair_back if paired else None,
    )
    grad_middle = grad_out + back_part

    grad_proj = norm_back(grad_middle, attn_unit, attn_scale, attention_gain).astype(BF16)
    attention_part = jnp.sum(grad_middle * attn_unit, axis=0)
    if paired:
        pair_gate_up, grad_proj = lax.optimization_barrier((pair_gate_up, grad_proj))
        away = [(own + pair).astype(BF16) for own, pair in zip(away, pair_weight_pieces(me ^ 1))]

    def attended_early(*groups):
        return [times_transposed(joined(group), output_weight).astype(BF16) for group in groups]

    grad_proj_groups, away, made = moves.gather(grad_proj, away, attended_early)
    if paired:
        got = [from_neighbour(part) for part in away]
    else:
        down_grad = scatter_rows(contract_rows(activated, row_of(grad_mlp_groups)).astype(BF16), 1)
        back = contract_rows(row_of(middle_groups), jnp.concatenate(grad_gate_up, axis=0))
        gate_up_grad = scatter_rows(back.astype(BF16), 0)
    grad_attended = row_of(made + attended_early(grad_proj_groups[-1]))
    output_part = sum(
        contract_rows(left, joined(right)) for left, right in zip(moves.groups(attended), grad_proj_groups)
    ).astype(BF16)
    output_grad = scatter_rows(output_part, 1)
    inner, grad_value, products, gain_parts = attend_back(
        shape, *tables, query, key, value, logsum, grad_attended.reshape(tensor, block, local)
    )
    place = lax.axis_index("tensor") * local
    spread = lax.dynamic_update_slice(jnp.zeros((2, width), F32), gain_parts, (0, place))
    spread = jnp.concatenate([spread, attention_part[None], feedforward_part[None]], axis=0)
    products = products.transpose(1, 0, 2).reshape(-1)
    packed = moves.add(jnp.concatenate([products, spread.reshape(-1)]).reshape(-1, 256)).reshape(-1)
    products = as_arrived(packed[: 2 * length].reshape(2, length)).T * (1.0 / width)
    gain_sums = add_rows(packed[2 * length :], rows)
    inner = inner.reshape(length, 2 * local)
    grad_qkv = [None, None, grad_value.reshape(length, local)]
    flat = as_arrived(sums).T
    for which in range(2):
        own = slice(which * local, (which + 1) * local)
        inverse = lax.rsqrt(flat[:, which : which + 1] * (1.0 / width) + norm_eps)
        unit = raw[:, own] * inverse
        grad_qkv[which] = (inverse * (inner[:, own] - unit * products[:, which : which + 1])).astype(BF16)
    grad_qkv = jnp.concatenate(grad_qkv, axis=1)
    qkv_part = contract_rows(hidden_all, grad_qkv).astype(BF16)
    grad_qkv, qkv_part = lax.optimization_barrier((grad_qkv, qkv_part))
    qkv_grad = scatter_rows(qkv_part, 0)

    def here(sent):
        nonlocal grad_mlp_groups, middle_groups, pair_grad_mlp_all, pair_middle_all, gain_sums
        grad_mlp_groups, middle_groups, pair_grad_mlp_all, pair_middle_all, gain_sums, _ = lax.optimization_barrier(
            (grad_mlp_groups, middle_groups, pair_grad_mlp_all, pair_middle_all, gain_sums, sent)
        )
        return [own + pair for own, pair in zip(own_weight_pieces(me), pair_weight_pieces(me))]

    input_part, kept, _ = moves.scatter(
        halves_of(grad_qkv), lambda part: times_transposed(part, weight_qkv), here if paired else None
    )
    input_grad = grad_middle + input_part
    if paired:
        got, output_grad, qkv_grad, input_grad = lax.optimization_barrier((got, output_grad, qkv_grad, input_grad))
        down_grad = kept[0] + got[0].astype(F32)
        gate_up_grad = kept[1] + got[1].astype(F32)
        near, two, three = gain_sums
        gain_sums = near + (two + three)
    gate_grad, up_grad = gate_up_grad[:, :hidden_units], gate_up_grad[:, hidden_units:]
    summed = gain_sums.reshape(4, width)
    return (
        result,
        input_grad,
        qkv_grad[:, :local],
        qkv_grad[:, local : 2 * local],
        qkv_grad[:, 2 * local :],
        output_grad,
        gate_grad,
        up_grad,
        down_grad,
        summed[0],
        summed[1],
        summed[2],
        summed[3],
    )


def solution(mesh):
    in_specs = (
        P(("dp", "tensor"), None),
        P("dp", None),
        P(None, "tensor"),
        P(None, "tensor"),
        P(None, "tensor"),
        P("tensor", None),
        P(None, "tensor"),
        P(None, "tensor"),
        P("tensor", None),
        P("tensor"),
        P("tensor"),
        P(),
        P(),
        P(("dp", "tensor"), None),
    )
    out_specs = (
        P(("dp", "tensor"), None),
        P(("dp", "tensor"), None),
        P("dp", "tensor"),
        P("dp", "tensor"),
        P("dp", "tensor"),
        P("tensor", "dp"),
        P("dp", "tensor"),
        P("dp", "tensor"),
        P("tensor", "dp"),
        P(),
        P(),
        P(),
        P(),
    )
    sizes = {axis: mesh.shape[axis] for axis in ("dp", "tensor")}
    return jax.shard_map(
        functools.partial(body, sizes), mesh=mesh, in_specs=in_specs, out_specs=out_specs, check_vma=False
    )
```

```python
import functools

import jax
import jax.numpy as jnp
from jax import lax
from jax.experimental import pallas as pl
from jax.experimental.pallas import tpu as pltpu
from jax.sharding import PartitionSpec as P

HEAD_DIM = 128
BF16 = jnp.bfloat16
F32 = jnp.float32

norm_eps = 1e-06
rope_base = 500000.0


def contract_rows(left, right):
    return lax.dot_general(left, right, (((0,), (0,)), ((), ())), preferred_element_type=F32)


def times_transposed(left, right):
    return lax.dot_general(left, right, (((1,), (1,)), ((), ())), preferred_element_type=F32)


def times(left, right):
    return jnp.dot(left, right, preferred_element_type=F32)


def rope_table(length, head_dim):
    half = head_dim // 2
    freq = rope_base ** (-(2.0 * jnp.arange(half, dtype=F32)) / head_dim)
    angle = jnp.arange(length, dtype=F32)[:, None] * freq[None, :]
    return jnp.concatenate([jnp.cos(angle), jnp.sin(angle)], axis=1)


def norm_back(grad, unit, inverse, gain):
    inner = grad * gain
    return inverse * (inner - unit * jnp.mean(inner * unit, axis=1, keepdims=True))


class PairedCores:
    def __init__(self):
        turn = lambda low, high: [(i, i ^ (low if i % 2 == 0 else high)) for i in range(8)]
        self.first, self.second, self.core = turn(2, 4), turn(4, 2), turn(1, 1)

    def send(self, value, way):
        return lax.ppermute(value, "tensor", way)

    def order(self):
        me = lax.axis_index("tensor")
        near = jnp.where(me % 2 == 0, 2, 4)
        far = 6 - near
        return jnp.stack([me ^ near, me ^ far, me, me ^ 6, me ^ 1 ^ far, me ^ 1 ^ near, me ^ 1, me ^ 7])

    def gather(self, own, meanwhile=None, early=None):
        first, second = self.send(own, self.first), self.send(own, self.second)
        other = self.send(own, self.core)
        if meanwhile is not None:
            second, meanwhile = lax.optimization_barrier((second, meanwhile))
        opposite = self.send(second, self.first)
        first_other, second_other = self.send(first, self.core), self.send(second, self.core)
        groups = [[own, other], [first, second, first_other, second_other]]
        made = None
        if early is not None:
            opposite, made = lax.optimization_barrier((opposite, early(*groups)))
        groups.append([opposite, self.send(opposite, self.core)])
        return groups, meanwhile, made

    def whole(self, groups):
        near, middle, last = groups
        if not isinstance(near, list):
            near, middle, last = jnp.split(near, 2), jnp.split(middle, 4), jnp.split(last, 2)
        first, second, first_other, second_other = middle
        return [first, second, near[0], last[0], first_other, second_other, near[1], last[1]]

    def groups(self, whole):
        first, second, own, opposite, first_other, second_other, other, opposite_other = jnp.split(whole, 8)
        groups = [[own, other], [first, second, first_other, second_other], [opposite, opposite_other]]
        return [jnp.concatenate(group, axis=0) for group in groups]

    def scatter(self, halves, product, meanwhile=None, late=None):
        mine, others = halves
        from_core = self.send(product(others).astype(BF16), self.core)
        own_part, from_core = lax.optimization_barrier((product(mine).astype(BF16), from_core))
        first, second, own, opposite = (
            part.astype(F32) + other.astype(F32)
            for part, other in zip(jnp.split(own_part, 4), jnp.split(from_core, 4))
        )
        sent = opposite.astype(BF16), first.astype(BF16)
        passing, from_first = (self.send(part, self.first) for part in sent)
        if meanwhile is not None:
            passing, meanwhile = lax.optimization_barrier((passing, meanwhile(sent)))
        from_second = self.send((second + passing.astype(F32)).astype(BF16), self.second)
        if late is not None:
            from_second, late = lax.optimization_barrier((from_second, late(passing)))
        return own + from_first.astype(F32) + from_second.astype(F32), meanwhile, late

    def add(self, value):
        for bit in (1, 2, 4):
            value = value + self.send(value, [(i, i ^ bit) for i in range(8)])
        return value


class AnyDevices:
    def __init__(self, size):
        self.size = size

    def order(self):
        return jnp.arange(self.size)

    def gather(self, own, meanwhile=None, early=None):
        return [[lax.all_gather(own, "tensor", axis=0, tiled=True)]], meanwhile, []

    def groups(self, whole):
        return [whole]

    def whole(self, groups):
        return groups[0] if isinstance(groups[0], list) else groups

    def scatter(self, halves, product, meanwhile=None, late=None):
        part = product(jnp.concatenate(halves, axis=0)).astype(BF16)
        total = lax.psum_scatter(part, "tensor", scatter_dimension=0, tiled=True).astype(F32)
        return total, meanwhile, late

    def add(self, value):
        return lax.psum(value, "tensor")


def in_pairs(step):
    return [(i, i ^ step) for i in range(4)]


def scatter_rows(part, dimension):
    return lax.psum_scatter(part, "dp", scatter_dimension=dimension, tiled=True).astype(F32)


def halve_rows(part, dimension):
    me = lax.axis_index("dp")
    away = [piece_of(part, dimension, me ^ step) for step in (1, 3)]
    kept = [piece_of(part, dimension, me ^ step) for step in (0, 2)]
    return kept, lax.ppermute(jnp.concatenate(away, axis=dimension), "dp", in_pairs(1))


def quarter_rows(halved, dimension):
    kept, got = halved
    own, other = (k.astype(F32) + g.astype(F32) for k, g in zip(kept, jnp.split(got, 2, axis=dimension)))
    return own, lax.ppermute(other.astype(BF16), "dp", in_pairs(2))


def piece_of(part, dimension, place):
    size = part.shape[dimension] // 4
    return lax.dynamic_slice_in_dim(part, place * size, size, dimension)


def add_rows(value, count):
    if count != 4:
        return lax.psum(value, "dp")
    one, two, three = (lax.ppermute(value, "dp", in_pairs(step)) for step in (1, 2, 3))
    return value, one, two, three


def turned(value):
    return pltpu.roll(value, HEAD_DIM // 2, 1)


def cosine_sine(table):
    lanes = lax.broadcasted_iota(jnp.int32, table.shape, 1)
    front, swapped = lanes < HEAD_DIM // 2, turned(table)
    return jnp.where(front, table, swapped), jnp.where(front, -swapped, table)


def scale_of(sums, at, width):
    return lax.rsqrt(sums[:, at : at + 1] * (1.0 / width) + norm_eps)


def window_of(b, block, back):
    first = jnp.maximum(b - back, 0)
    return first, pl.ds(pl.multiple_of(first * block, block), (back + 1) * block)


def allowed_in(docs, ahead, block, back):
    docs_row, docs_col = docs[:1, :], docs[:, :block].T[:, 1:2]
    window = (back + 1) * block
    rows = lax.broadcasted_iota(jnp.int32, (block, window), 0) + ahead * block
    columns = lax.broadcasted_iota(jnp.int32, (block, window), 1)
    return (docs_col == docs_row) & (columns <= rows)


def put_in_row(groups, row):
    block = row.shape[1]
    if len(groups) == 1:
        for at in range(row.shape[0]):
            row[at] = groups[0][at * block : (at + 1) * block, :]
        return
    near, beside, last = groups
    places = (beside, 0), (beside, 1), (near, 0), (last, 0), (beside, 2), (beside, 3), (near, 1), (last, 1)
    for at, (group, place) in enumerate(places):
        row[at] = group[place * block : (place + 1) * block, :]


def attend_kernel(
    shape,
    count,
    order,
    *refs,
):
    raws, refs = refs[:count], refs[count:]
    attend_body(shape, order, raws, *refs)


def attend_body(
    shape,
    order,
    raws,
    sums,
    gains,
    table,
    docs,
    attended,
    query,
    key,
    value,
    logsum,
    keys,
    values,
    raw,
):
    blocks, block, width, local, back, scale = shape
    heads = local // HEAD_DIM
    b = pl.program_id(0)

    @pl.when(b == 0)
    def _():
        put_in_row(raws, raw)
        keys[...] = jnp.zeros(keys.shape, BF16)
        values[...] = jnp.zeros(values.shape, BF16)

    total = sums[0].T
    cos, sin = cosine_sine(table[...])
    for which in range(2):
        inverse = scale_of(total, which, width)
        for h in range(heads):
            lanes = slice(h * HEAD_DIM, (h + 1) * HEAD_DIM)
            own = slice(which * local + h * HEAD_DIM, which * local + (h + 1) * HEAD_DIM)
            v = raw[order[b], :, own] * inverse * gains[which : which + 1, lanes]
            (query, key)[which][:, lanes] = (v * cos + turned(v) * sin).astype(BF16)
    value[...] = raw[order[b], :, 2 * local :].astype(BF16)
    now = pl.ds(pl.multiple_of(b * block, block), block)
    keys[now, :] = key[...]
    values[now, :] = value[...]
    first, window = window_of(b, block, back)
    allowed = allowed_in(docs[0], b - first, block, back)
    logsums = []
    for h in range(heads):
        lanes = slice(h * HEAD_DIM, (h + 1) * HEAD_DIM)
        scores = times_transposed(query[:, lanes], keys[window, lanes]) * scale
        scores = jnp.where(allowed, scores, -1e30)
        top = jnp.max(scores, axis=1, keepdims=True)
        weights = jnp.exp(scores - top)
        mass = jnp.sum(weights, axis=1, keepdims=True)
        shares = (weights * (1.0 / mass)).astype(BF16)
        attended[0, :, lanes] = times(shares, values[window, lanes]).astype(BF16)
        logsums.append(top + jnp.log(mass))
    logsum[0] = jnp.concatenate(logsums, axis=1).T


def attend_back_kernel(
    shape,
    order,
    raw,
    sums,
    gains,
    table,
    docs,
    query,
    keys,
    values,
    logsum,
    *refs,
):
    grads = refs[:-8]
    inner, grad_value, products, gain_parts, grad_query_sum, grad_key_sum, grad_value_sum, grad = refs[-8:]
    blocks, block, width, local, back, scale = shape
    heads = local // HEAD_DIM
    b = pl.program_id(0)

    @pl.when(b == 0)
    def _():
        put_in_row(grads, grad)
        grad_key_sum[...] = jnp.zeros(grad_key_sum.shape, F32)
        grad_value_sum[...] = jnp.zeros(grad_value_sum.shape, F32)
        gain_parts[...] = jnp.zeros(gain_parts.shape, F32)

    @pl.when(b < blocks)
    def _():
        first, window = window_of(b, block, back)
        allowed = allowed_in(docs[0], b - first, block, back)
        now = pl.ds(pl.multiple_of(b * block, block), block)
        tops = logsum[0].T
        for h in range(heads):
            lanes = slice(h * HEAD_DIM, (h + 1) * HEAD_DIM)
            q, k, v, g = query[:, lanes], keys[window, lanes], values[window, lanes], grad[order[b], :, lanes]
            scores = times_transposed(q, k) * scale
            chances = jnp.exp(jnp.where(allowed, scores, -1e30) - tops[:, h : h + 1])
            grad_shares = times_transposed(g, v)
            offset = jnp.sum(chances * grad_shares, axis=1, keepdims=True)
            grad_scores = (chances * (grad_shares - offset)).astype(BF16)
            grad_query_sum[now, lanes] = times(grad_scores, k) * scale
            grad_key_sum[window, lanes] += contract_rows(grad_scores, q) * scale
            grad_value_sum[window, lanes] += contract_rows(chances.astype(BF16), g)

    @pl.when(b >= back)
    def _():
        rows = pl.ds(pl.multiple_of((b - back) * block, block), block)
        total = sums[0].T
        cos, sin = cosine_sine(table[...])
        grad_value[0] = grad_value_sum[rows, :].astype(BF16)
        all_dots = []
        for which in range(2):
            inverse = scale_of(total, which, width)
            dots = jnp.zeros((block, 1), F32)
            for h in range(heads):
                lanes = slice(h * HEAD_DIM, (h + 1) * HEAD_DIM)
                own = slice(which * local + h * HEAD_DIM, which * local + (h + 1) * HEAD_DIM)
                unit = raw[0, :, own] * inverse
                g = (grad_query_sum, grad_key_sum)[which][rows, lanes]
                g = g * cos + turned(g * sin)
                gain_parts[which : which + 1, lanes] += jnp.sum(g * unit, axis=0, keepdims=True)
                c = g * gains[which : which + 1, lanes]
                inner[0, :, own] = c
                dots = dots + jnp.sum(c * unit, axis=1, keepdims=True)
            all_dots.append(dots)
        products[0] = jnp.concatenate(all_dots, axis=1).T


def attend(shape, order, raws, sums, gains, table, docs):
    blocks, block, width, local, back, scale = shape
    heads, length = local // HEAD_DIM, blocks * block
    in_row = lambda columns: pl.BlockSpec((block, columns), lambda b, order: (b, 0))
    arrived = lambda columns: pl.BlockSpec((1, block, columns), lambda b, order: (order[b], 0, 0))
    return pl.pallas_call(
        functools.partial(attend_kernel, shape, len(raws)),
        out_shape=(
            jax.ShapeDtypeStruct((blocks, block, local), BF16),
            jax.ShapeDtypeStruct((length, local), BF16),
            jax.ShapeDtypeStruct((length, local), BF16),
            jax.ShapeDtypeStruct((length, local), BF16),
            jax.ShapeDtypeStruct((blocks, heads, block), F32),
        ),
        grid_spec=pltpu.PrefetchScalarGridSpec(
            num_scalar_prefetch=1,
            grid=(blocks,),
            in_specs=[pl.BlockSpec(raw.shape, lambda b, order: (0, 0)) for raw in raws]
            + [
                pl.BlockSpec((1, 2, block), lambda b, order: (b, 0, 0)),
                pl.BlockSpec((2, local), lambda b, order: (0, 0)),
                in_row(HEAD_DIM),
                pl.BlockSpec((1, 2, (back + 1) * block), lambda b, order: (b, 0, 0)),
            ],
            out_specs=(
                arrived(local),
                in_row(local),
                in_row(local),
                in_row(local),
                pl.BlockSpec((1, heads, block), lambda b, order: (b, 0, 0)),
            ),
            scratch_shapes=[pltpu.VMEM((length, local), BF16)] * 2 + [pltpu.VMEM((blocks, block, 3 * local), F32)],
        ),
        compiler_params=pltpu.CompilerParams(vmem_limit_bytes=30 * 2**20),
        cost_estimate=pl.CostEstimate(flops=4 * 10**9, bytes_accessed=10**7, transcendentals=2 * 10**6),
    )(order, *raws, sums, gains, table, docs)


def attend_back(shape, order, raw, sums, gains, table, docs, query, key, value, logsum, grads):
    blocks, block, width, local, back, scale = shape
    heads, length = local // HEAD_DIM, blocks * block
    now = lambda b: jnp.minimum(b, blocks - 1)
    done = lambda b: jnp.maximum(b - back, 0)
    whole = pl.BlockSpec((length, local), lambda b, order: (0, 0))
    finished = lambda columns: pl.BlockSpec((1, block, columns), lambda b, order: (order[done(b)], 0, 0))
    return pl.pallas_call(
        functools.partial(attend_back_kernel, shape),
        out_shape=(
            jax.ShapeDtypeStruct((blocks, block, 2 * local), F32),
            jax.ShapeDtypeStruct((blocks, block, local), BF16),
            jax.ShapeDtypeStruct((blocks, 2, block), F32),
            jax.ShapeDtypeStruct((2, local), F32),
        ),
        grid_spec=pltpu.PrefetchScalarGridSpec(
            num_scalar_prefetch=1,
            grid=(blocks + back,),
            in_specs=[
                finished(3 * local),
                pl.BlockSpec((1, 2, block), lambda b, order: (done(b), 0, 0)),
                pl.BlockSpec((2, local), lambda b, order: (0, 0)),
                pl.BlockSpec((block, HEAD_DIM), lambda b, order: (done(b), 0)),
                pl.BlockSpec((1, 2, (back + 1) * block), lambda b, order: (now(b), 0, 0)),
                pl.BlockSpec((block, local), lambda b, order: (now(b), 0)),
                whole,
                whole,
                pl.BlockSpec((1, heads, block), lambda b, order: (now(b), 0, 0)),
            ]
            + [pl.BlockSpec(grad.shape, lambda b, order: (0, 0)) for grad in grads],
            out_specs=(
                finished(2 * local),
                finished(local),
                pl.BlockSpec((1, 2, block), lambda b, order: (done(b), 0, 0)),
                pl.BlockSpec((2, local), lambda b, order: (0, 0)),
            ),
            scratch_shapes=[pltpu.VMEM((length, local), F32)] * 3 + [pltpu.VMEM((blocks, block, local), BF16)],
        ),
        compiler_params=pltpu.CompilerParams(vmem_limit_bytes=28 * 2**20),
        cost_estimate=pl.CostEstimate(flops=8 * 10**9, bytes_accessed=2 * 10**7, transcendentals=2 * 10**6),
    )(order, raw, sums, gains, table, docs, query, key, value, logsum, *grads)


TILE = 256


def gated_grad(grad_act, gate, up):
    sigma = jax.nn.sigmoid(gate)
    grad_gate = grad_act * up * sigma * (1.0 + gate * (1.0 - sigma))
    return grad_gate.astype(BF16), (grad_act * gate * sigma).astype(BF16)


def feed_back_kernel(count, with_activated, *refs):
    grads, (weight, both) = refs[:count], refs[count : count + 2]
    *_, mine, others, rows = refs
    activated = refs[-4] if with_activated else None
    block, tile = grads[0].shape[0], weight.shape[0]
    units, half = mine.shape[-1] // 2, rows.shape[0] // 2
    j = pl.program_id(0)

    @pl.when(j == 0)
    def _():
        for at, grad in enumerate(grads):
            rows[at * block : (at + 1) * block, :] = grad[...]

    start = pl.multiple_of(j * tile, tile)
    gate, up = (both[:, pl.ds(at, tile)].astype(F32) for at in (start, start + units))
    if activated is not None:
        activated[...] = (gate * jax.nn.sigmoid(gate) * up).astype(BF16)
    grad_act = times_transposed(rows[...], weight[...])
    for at, part in zip((start, start + units), gated_grad(grad_act, gate, up)):
        for out, own in ((mine, part[:half]), (others, part[half:])):
            out[:, :, pl.ds(at, tile)] = own.reshape(out.shape[:2] + (tile,))


def feed_back(grads, down_weight, both, slot, slots, before=(), with_activated=False):
    count, width = len(grads), grads[0].shape[1]
    units, tile = down_weight.shape[0], min(TILE, down_weight.shape[0])
    tiles, rows = units // tile, sum(grad.shape[0] for grad in grads)
    once = lambda shape: pl.BlockSpec(shape, lambda j: (0, 0), pipeline_mode=pl.Buffered(1))
    in_specs = [once(grad.shape) for grad in grads]
    in_specs += [pl.BlockSpec((tile, width), lambda j: (j, 0)), once(both.shape)]
    in_specs += [pl.BlockSpec(memory_space=pl.ANY)] * len(before)
    args = [*grads, down_weight, both, *before]
    part = rows // (2 * slots)
    extra_shape, extra_spec = (), ()
    if with_activated:
        extra_shape = (jax.ShapeDtypeStruct((rows, units), BF16),)
        extra_spec = (pl.BlockSpec((rows, tile), lambda j: (0, j)),)
    return pl.pallas_call(
        functools.partial(feed_back_kernel, count, with_activated),
        grid=(tiles,),
        out_shape=extra_shape + (jax.ShapeDtypeStruct((4, part, 2 * units), BF16),) * 2,
        in_specs=in_specs,
        out_specs=extra_spec + (pl.BlockSpec((slots, part, 2 * units), lambda j: (slot // slots, 0, 0)),) * 2,
        scratch_shapes=[pltpu.VMEM((rows, width), BF16)],
        input_output_aliases={count + 2 + at: at for at in range(len(before))},
        compiler_params=pltpu.CompilerParams(vmem_limit_bytes=(8 + 7 * rows // 192) * 2**20),
        cost_estimate=pl.CostEstimate(
            flops=2 * rows * width * units,
            bytes_accessed=2 * units * width + 12 * rows * units + 2 * rows * width,
            transcendentals=rows * units,
        ),
    )(*args)


def pieces_kernel(plan, count, place, *refs):
    sources, outs, sems = refs[:count], refs[count:-1], refs[-1]
    copies = []
    for out, parts in zip(outs, plan):
        size = out.shape[1]
        columns = pl.ds(pl.multiple_of(place[0] * size, size), size)
        at = 0
        for source, start, rows in parts:
            copies.append(
                pltpu.make_async_copy(
                    sources[source].at[pl.ds(start, rows), columns],
                    out.at[pl.ds(at, rows), :],
                    sems.at[len(copies)],
                )
            )
            at += rows
    for copy in copies:
        copy.start()
    for copy in copies:
        copy.wait()


def pieces_of(sources, plan, place, count=4):
    size = sources[0].shape[1] // count
    shapes = [(sum(rows for _, _, rows in parts), size) for parts in plan]
    return pl.pallas_call(
        functools.partial(pieces_kernel, plan, len(sources)),
        out_shape=[jax.ShapeDtypeStruct(shape, BF16) for shape in shapes],
        in_specs=[pl.BlockSpec(memory_space=pltpu.SMEM)] + [pl.BlockSpec(memory_space=pltpu.HBM)] * len(sources),
        out_specs=[pl.BlockSpec(memory_space=pltpu.HBM)] * len(plan),
        scratch_shapes=[pltpu.SemaphoreType.DMA((sum(len(parts) for parts in plan),))],
        compiler_params=pltpu.CompilerParams(vmem_limit_bytes=2**20),
        cost_estimate=pl.CostEstimate(
            flops=0, bytes_accessed=sum(4 * rows * columns for rows, columns in shapes), transcendentals=0
        ),
    )(jnp.reshape(place, (1,)).astype(jnp.int32), *sources)


def joined_rows(blocks):
    return pieces_of(blocks, [[(at, 0, block.shape[0]) for at, block in enumerate(blocks)]], 0, 1)[0]


def body(
    sizes,
    hidden_in,
    doc_ids,
    query_weight,
    key_weight,
    value_weight,
    output_weight,
    gate_weight,
    up_weight,
    down_weight,
    query_gain,
    key_gain,
    attention_gain,
    feedforward_gain,
    out_grad,
):
    tensor, rows = sizes["tensor"], sizes["dp"]
    moves = PairedCores() if tensor == 8 else AnyDevices(tensor)
    width = hidden_in.shape[1]
    local = query_weight.shape[1]
    hidden_units = gate_weight.shape[1]
    documents = doc_ids[0]
    length = documents.shape[0]
    block = length // tensor
    most = length // 4
    back = -(-(most - 1) // block)
    shape = (tensor, block, width, local, back, HEAD_DIM ** (-0.5))

    places = moves.order()
    steps = jnp.arange(tensor, dtype=jnp.int32)
    meets = places[None, :] == steps[:, None]
    order = jnp.sum(jnp.where(meets, steps[None, :], 0), axis=1)

    def in_row(value):
        parts = value.reshape(1, 2, tensor, block)
        return jnp.sum(jnp.where(meets[:, None, :, None], parts, 0.0), axis=2)

    def as_arrived(value):
        parts = value.transpose(1, 0, 2)[:, :, None]
        return jnp.sum(jnp.where(meets[None, :, :, None], parts, 0.0), axis=1).reshape(2, length)

    table = rope_table(length, HEAD_DIM)
    firsts = [max(b - back, 0) * block for b in range(tensor)]
    numbers = documents.astype(F32)
    docs = jnp.stack([numbers[first : first + (back + 1) * block] for first in firsts])
    own_docs = jnp.pad(numbers.reshape(tensor, block), ((0, 0), (0, back * block)))
    docs = jnp.stack([docs, own_docs], axis=1)
    gains = jnp.stack([query_gain, key_gain])

    def row_of(groups):
        return jnp.concatenate(moves.whole(groups), axis=0)

    def joined(group):
        return jnp.concatenate(group, axis=0)

    weight_qkv = jnp.concatenate([query_weight, key_weight, value_weight], axis=1)
    weight_gate_up = jnp.concatenate([gate_weight, up_weight], axis=1)
    paired = rows == 4 and tensor == 8

    def halves_of(whole):
        return jnp.split(whole, 2)

    def raw_of(*groups):
        return [times(joined(group), weight_qkv) for group in groups]

    hidden_groups, _, raw = moves.gather(hidden_in, early=raw_of)
    raw = raw + raw_of(hidden_groups[-1])
    squares = jnp.stack(
        [
            row_of([jnp.sum(jnp.square(part[:, at : at + local]), axis=1) for part in raw])
            for at in (0, local)
        ]
    )
    raws, raw = raw, row_of(raw)
    sums = moves.add(in_row(squares))
    tables = (sums, gains, table, docs)
    attended_blocks, query, key, value, logsum = attend(shape, order, raws, *tables)
    attended = attended_blocks.reshape(length, local)
    def join_hidden(passing):
        groups, _ = lax.optimization_barrier((hidden_groups, passing))
        return joined_rows(moves.whole(groups))

    attn_proj, _, hidden_all = moves.scatter(
        halves_of(attended),
        lambda part: times(part, output_weight),
        late=join_hidden if tensor == 8 else None,
    )
    if tensor != 8:
        hidden_all = hidden_groups[0][0]
    attn_scale = lax.rsqrt(jnp.mean(attn_proj * attn_proj, axis=1, keepdims=True) + norm_eps)
    attn_unit = attn_proj * attn_scale
    middle = hidden_in.astype(F32) + attn_unit * attention_gain
    middle_low = middle.astype(BF16)

    def activate(both):
        gate, up = both[:, :hidden_units], both[:, hidden_units:]
        return (gate * jax.nn.sigmoid(gate) * up).astype(BF16)

    def both_of(*groups):
        both = [times(joined(group), weight_gate_up) for group in groups]
        return both, [activate(part) for part in both]

    def to_pair(value):
        return lax.ppermute(value, "dp", in_pairs(2))

    def gather_pair(value):
        return lax.all_gather(value, "tensor", axis=0, tiled=True)

    pair_middle = to_pair(middle_low) if paired else None

    def both_early(*groups):
        return both_of(*groups), pair_middle

    middle_groups, _, made = moves.gather(middle_low, early=both_early)
    made, pair_middle = made or (([], []), None)
    if paired:
        pair_middle_all = gather_pair(pair_middle)
    both_groups, activated = (early + late for early, late in zip(made, both_of(middle_groups[-1])))
    activated = lax.optimization_barrier(row_of(activated))
    mlp_proj, _, _ = moves.scatter(halves_of(activated), lambda part: times(part, down_weight))
    mlp_scale = lax.rsqrt(jnp.mean(mlp_proj * mlp_proj, axis=1, keepdims=True) + norm_eps)
    mlp_unit = mlp_proj * mlp_scale
    result = middle + mlp_unit * feedforward_gain

    grad_out = out_grad.astype(F32)
    grad_mlp = norm_back(grad_out, mlp_unit, mlp_scale, feedforward_gain).astype(BF16)
    feedforward_part = jnp.sum(grad_out * mlp_unit, axis=0)
    pair_both = None
    if paired:
        pair_middle_all, grad_mlp = lax.optimization_barrier((pair_middle_all, grad_mlp))
        pair_both = times(pair_middle_all, weight_gate_up).astype(BF16)

    def back_early(near, beside):
        part = feed_back(near, down_weight, both_groups[0], 2, 1)
        part = feed_back(beside, down_weight, both_groups[1], 0, 2, part)
        return part, pair_grad_mlp[1]

    pair_grad_mlp = [None, None]
    if paired:
        first_half, second_half = jnp.split(grad_mlp, 2, axis=1)
        first_half, second_half = lax.optimization_barrier((to_pair(first_half), second_half))
        pair_grad_mlp = [first_half, to_pair(second_half)]
    meanwhile = (pair_both, pair_grad_mlp[0])
    grad_mlp_groups, (pair_both, first_half), made = moves.gather(grad_mlp, meanwhile, back_early)
    if tensor == 8:
        made, second_half = made
        grad_gate_up = feed_back(grad_mlp_groups[-1], down_weight, both_groups[2], 3, 1, made)
        grad_gate_up = [half.reshape(length // 2, 2 * hidden_units) for half in grad_gate_up]
    else:
        grad_act = times_transposed(grad_mlp_groups[0][0], down_weight)
        both = both_groups[0].astype(F32)
        grad_gate_up = gated_grad(grad_act, both[:, :hidden_units], both[:, hidden_units:])
        grad_gate_up = halves_of(jnp.concatenate(grad_gate_up, axis=1))
    if paired:
        pair_grad_mlp_all = gather_pair(jnp.concatenate([first_half, second_half], axis=1))

    me = lax.axis_index("dp")
    half_rows = length // 2

    def own_weight_pieces(place):
        blocks = moves.whole(middle_groups) + moves.whole(grad_mlp_groups)
        part = [(at, 0, block) for at in range(16)]
        mine, others, grads = pieces_of(blocks, [part[:4], part[4:8], part[8:]], place)
        return [
            contract_rows(grads, activated),
            contract_rows(mine, grad_gate_up[0]) + contract_rows(others, grad_gate_up[1]),
        ]

    def pair_weight_pieces(place):
        plan = [[(0, 0, half_rows)], [(0, half_rows, half_rows)], [(1, 0, length)]]
        first, second, grads = pieces_of([pair_middle_all, pair_grad_mlp_all], plan, place)
        return [
            contract_rows(grads, pair_activated),
            contract_rows(first, pair_gate_up[0]) + contract_rows(second, pair_gate_up[1]),
        ]

    def gate_up_own(place):
        part = [(at, 0, block) for at in range(8)]
        mine, others = pieces_of(moves.whole(middle_groups), [part[:4], part[4:]], place)
        return contract_rows(mine, grad_gate_up[0]) + contract_rows(others, grad_gate_up[1])

    def gate_up_pair(place):
        plan = [[(0, 0, half_rows)], [(0, half_rows, half_rows)]]
        first, second = pieces_of([pair_middle_all], plan, place)
        return contract_rows(first, pair_gate_up[0]) + contract_rows(second, pair_gate_up[1])

    def down_pieces(place):
        part = [(at, 0, block) for at in range(8)]
        blocks = moves.whole(grad_mlp_groups) + [pair_grad_mlp_all]
        own, pair = pieces_of(blocks, [part, [(8, 0, length)]], place)
        return contract_rows(own, activated) + contract_rows(pair, pair_activated)

    def own_away(sent):
        nonlocal grad_mlp_groups, middle_groups
        grad_mlp_groups, middle_groups, _ = lax.optimization_barrier((grad_mlp_groups, middle_groups, sent))
        return own_weight_pieces(me ^ 1)

    def pair_back(passing):
        grads, _ = lax.optimization_barrier((pair_grad_mlp_all, passing))
        pair_activated, *pair_gate_up = feed_back([grads], down_weight, pair_both, 0, 4, with_activated=True)
        return pair_activated, [half.reshape(half_rows, 2 * hidden_units) for half in pair_gate_up]

    back_part, away, pair_gate_up = moves.scatter(
        grad_gate_up,
        lambda part: times_transposed(part, weight_gate_up),
        own_away if paired else None,
        pair_back if paired else None,
    )
    grad_middle = grad_out + back_part

    grad_proj = norm_back(grad_middle, attn_unit, attn_scale, attention_gain).astype(BF16)
    attention_part = jnp.sum(grad_middle * attn_unit, axis=0)
    if paired:
        (pair_activated, pair_gate_up), grad_proj = lax.optimization_barrier((pair_gate_up, grad_proj))
        away = [(own + pair).astype(BF16) for own, pair in zip(away, pair_weight_pieces(me ^ 1))]
        away = [away[0], *jnp.split(away[1], 2, axis=1)]
        away = [half for part in away for half in jnp.split(part, 2)]
        got = [lax.ppermute(part, "dp", in_pairs(1)) for part in away]

    def attended_early(*groups):
        return [times_transposed(joined(group), output_weight).astype(BF16) for group in groups]

    def proj_early(*groups):
        if not paired:
            return attended_early(*groups), None, None
        return attended_early(*groups), got[0], gate_up_own(me)

    grad_proj_groups, away, made = moves.gather(grad_proj, away, proj_early)
    made, *rest = made or ([],)
    if paired:
        got[0], kept_gate_up = rest
    else:
        down_grad = scatter_rows(contract_rows(activated, row_of(grad_mlp_groups)).astype(BF16), 1)
        back = contract_rows(row_of(middle_groups), jnp.concatenate(grad_gate_up, axis=0))
        gate_grad, up_grad = jnp.split(scatter_rows(back.astype(BF16), 0), 2, axis=1)
    grad_attended = made + attended_early(grad_proj_groups[-1])
    raw_blocks = raw.reshape(tensor, block, 3 * local)
    inner, grad_value, products, gain_parts = attend_back(
        shape, order, raw_blocks, *tables, query, key, value, logsum, grad_attended
    )
    if paired:
        (products, grad_proj_groups), *got[1:3] = lax.optimization_barrier(
            ((products, grad_proj_groups), *got[1:3])
        )
    output_part = sum(
        contract_rows(joined(right), left) for left, right in zip(moves.groups(attended), grad_proj_groups)
    )
    place = lax.axis_index("tensor") * local
    spread = lax.dynamic_update_slice(jnp.zeros((2, width), F32), gain_parts, (0, place))
    spread = jnp.concatenate([spread, attention_part[None], feedforward_part[None]], axis=0)
    packed = moves.add(jnp.concatenate([products.reshape(-1), spread.reshape(-1)]).reshape(-1, 256))
    if paired:
        packed, got[3] = lax.optimization_barrier((packed, got[3]))
    packed = packed.reshape(-1)
    products = as_arrived(packed[: 2 * length].reshape(tensor, 2, block)).T * (1.0 / width)
    gain_sums = add_rows(packed[2 * length :], rows)
    inner = inner.reshape(length, 2 * local)
    grad_qkv = [None, None, grad_value.reshape(length, local)]
    flat = as_arrived(sums).T
    for which in range(2):
        own = slice(which * local, (which + 1) * local)
        inverse = lax.rsqrt(flat[:, which : which + 1] * (1.0 / width) + norm_eps)
        unit = raw[:, own] * inverse
        grad_qkv[which] = (inverse * (inner[:, own] - unit * products[:, which : which + 1])).astype(BF16)
    grad_qkv = jnp.concatenate(grad_qkv, axis=1)
    qkv_part = contract_rows(hidden_all, grad_qkv)
    projections_part = jnp.concatenate([qkv_part, output_part], axis=1).astype(BF16)
    if paired:
        projections_part, got[4] = lax.optimization_barrier((projections_part, got[4]))
    grad_qkv, projections_part = lax.optimization_barrier((grad_qkv, projections_part))
    projections_grad = scatter_rows(projections_part, 0)

    def finish_gate_up(sent):
        nonlocal pair_middle_all, pair_gate_up
        values, _ = lax.optimization_barrier(((pair_middle_all, pair_gate_up, got[5]), sent))
        pair_middle_all, pair_gate_up, got[5] = values
        kept = kept_gate_up + gate_up_pair(me)
        gate_got, up_got = (jnp.concatenate(parts, axis=0).astype(F32) for parts in (got[2:4], got[4:]))
        return kept[:, :hidden_units] + gate_got, kept[:, hidden_units:] + up_got

    def finish_down(passing):
        nonlocal grad_mlp_groups, pair_grad_mlp_all
        values, _ = lax.optimization_barrier(((grad_mlp_groups, pair_grad_mlp_all), passing))
        grad_mlp_groups, pair_grad_mlp_all = values
        return (down_pieces(me) + jnp.concatenate(got[:2], axis=0).astype(F32)).T

    input_part, made, down_made = moves.scatter(
        halves_of(grad_qkv),
        lambda part: times_transposed(part, weight_qkv),
        finish_gate_up if paired else None,
        finish_down if paired else None,
    )
    input_grad = grad_middle + input_part
    if paired:
        (gate_grad, up_grad), down_grad = made, down_made
        results = input_grad, down_grad, gate_grad, up_grad
        gain_sums, results = lax.optimization_barrier((gain_sums, results))
        input_grad, down_grad, gate_grad, up_grad = results
        own, one, two, three = gain_sums
        gain_sums = (own + one) + (two + three)
    output_grad = projections_grad[:, 3 * local :].T
    summed = gain_sums.reshape(4, width)
    return (
        result,
        input_grad,
        projections_grad[:, :local],
        projections_grad[:, local : 2 * local],
        projections_grad[:, 2 * local : 3 * local],
        output_grad,
        gate_grad,
        up_grad,
        down_grad,
        summed[0],
        summed[1],
        summed[2],
        summed[3],
    )


def solution(mesh):
    in_specs = (
        P(("dp", "tensor"), None),
        P("dp", None),
        P(None, "tensor"),
        P(None, "tensor"),
        P(None, "tensor"),
        P("tensor", None),
        P(None, "tensor"),
        P(None, "tensor"),
        P("tensor", None),
        P("tensor"),
        P("tensor"),
        P(),
        P(),
        P(("dp", "tensor"), None),
    )
    out_specs = (
        P(("dp", "tensor"), None),
        P(("dp", "tensor"), None),
        P("dp", "tensor"),
        P("dp", "tensor"),
        P("dp", "tensor"),
        P("tensor", "dp"),
        P("dp", "tensor"),
        P("dp", "tensor"),
        P("tensor", "dp"),
        P(),
        P(),
        P(),
        P(),
    )
    sizes = {axis: mesh.shape[axis] for axis in ("dp", "tensor")}
    return jax.shard_map(
        functools.partial(body, sizes), mesh=mesh, in_specs=in_specs, out_specs=out_specs, check_vma=False
    )
```

```python
import functools

import jax
import jax.numpy as jnp
from jax import lax
from jax.experimental import pallas as pl
from jax.experimental.pallas import tpu as pltpu
from jax.sharding import PartitionSpec as P

HEAD_DIM = 128
BF16 = jnp.bfloat16
F32 = jnp.float32

norm_eps = 1e-06
rope_base = 500000.0


def contract_rows(left, right):
    return lax.dot_general(left, right, (((0,), (0,)), ((), ())), preferred_element_type=F32)


def times_transposed(left, right):
    return lax.dot_general(left, right, (((1,), (1,)), ((), ())), preferred_element_type=F32)


def times(left, right):
    return jnp.dot(left, right, preferred_element_type=F32)


def rope_table(length, head_dim):
    half = head_dim // 2
    freq = rope_base ** (-(2.0 * jnp.arange(half, dtype=F32)) / head_dim)
    angle = jnp.arange(length, dtype=F32)[:, None] * freq[None, :]
    return jnp.concatenate([jnp.cos(angle), jnp.sin(angle)], axis=1)


def norm_back(grad, unit, inverse, gain):
    inner = grad * gain
    return inverse * (inner - unit * jnp.mean(inner * unit, axis=1, keepdims=True))


class PairedCores:
    def __init__(self):
        turn = lambda low, high: [(i, i ^ (low if i % 2 == 0 else high)) for i in range(8)]
        self.first, self.second, self.core = turn(2, 4), turn(4, 2), turn(1, 1)

    def send(self, value, way):
        return lax.ppermute(value, "tensor", way)

    def order(self):
        me = lax.axis_index("tensor")
        near = jnp.where(me % 2 == 0, 2, 4)
        far = 6 - near
        return jnp.stack([me ^ near, me ^ far, me, me ^ 6, me ^ 1 ^ far, me ^ 1 ^ near, me ^ 1, me ^ 7])

    def gather(self, own, meanwhile=None, early=None):
        first, second = self.send(own, self.first), self.send(own, self.second)
        other = self.send(own, self.core)
        if meanwhile is not None:
            second, meanwhile = lax.optimization_barrier((second, meanwhile))
        opposite = self.send(second, self.first)
        first_other, second_other = self.send(first, self.core), self.send(second, self.core)
        groups = [[own, other], [first, second, first_other, second_other]]
        made = None
        if early is not None:
            opposite, made = lax.optimization_barrier((opposite, early(*groups)))
        groups.append([opposite, self.send(opposite, self.core)])
        return groups, meanwhile, made

    def whole(self, groups):
        near, middle, last = groups
        if not isinstance(near, list):
            near, middle, last = jnp.split(near, 2), jnp.split(middle, 4), jnp.split(last, 2)
        first, second, first_other, second_other = middle
        return [first, second, near[0], last[0], first_other, second_other, near[1], last[1]]

    def groups(self, whole):
        first, second, own, opposite, first_other, second_other, other, opposite_other = jnp.split(whole, 8)
        groups = [[own, other], [first, second, first_other, second_other], [opposite, opposite_other]]
        return [jnp.concatenate(group, axis=0) for group in groups]

    def scatter(self, halves, product, meanwhile=None, late=None):
        mine, others = halves
        from_core = self.send(product(others).astype(BF16), self.core)
        own_part, from_core = lax.optimization_barrier((product(mine).astype(BF16), from_core))
        first, second, own, opposite = (
            part.astype(F32) + other.astype(F32)
            for part, other in zip(jnp.split(own_part, 4), jnp.split(from_core, 4))
        )
        sent = opposite.astype(BF16), first.astype(BF16)
        passing, from_first = (self.send(part, self.first) for part in sent)
        if meanwhile is not None:
            passing, meanwhile = lax.optimization_barrier((passing, meanwhile(sent)))
        from_second = self.send((second + passing.astype(F32)).astype(BF16), self.second)
        if late is not None:
            from_second, late = lax.optimization_barrier((from_second, late(passing)))
        return own + from_first.astype(F32) + from_second.astype(F32), meanwhile, late

    def add(self, value):
        for bit in (1, 2, 4):
            value = value + self.send(value, [(i, i ^ bit) for i in range(8)])
        return value


class AnyDevices:
    def __init__(self, size):
        self.size = size

    def order(self):
        return jnp.arange(self.size)

    def gather(self, own, meanwhile=None, early=None):
        return [[lax.all_gather(own, "tensor", axis=0, tiled=True)]], meanwhile, []

    def groups(self, whole):
        return [whole]

    def whole(self, groups):
        return groups[0] if isinstance(groups[0], list) else groups

    def scatter(self, halves, product, meanwhile=None, late=None):
        part = product(jnp.concatenate(halves, axis=0)).astype(BF16)
        total = lax.psum_scatter(part, "tensor", scatter_dimension=0, tiled=True).astype(F32)
        return total, meanwhile, late

    def add(self, value):
        return lax.psum(value, "tensor")


def in_pairs(step):
    return [(i, i ^ step) for i in range(4)]


def scatter_rows(part, dimension):
    return lax.psum_scatter(part, "dp", scatter_dimension=dimension, tiled=True)


def halve_rows(part, dimension):
    me = lax.axis_index("dp")
    away = [piece_of(part, dimension, me ^ step) for step in (1, 3)]
    kept = [piece_of(part, dimension, me ^ step) for step in (0, 2)]
    return kept, lax.ppermute(jnp.concatenate(away, axis=dimension), "dp", in_pairs(1))


def quarter_rows(halved, dimension):
    kept, got = halved
    own, other = (k.astype(F32) + g.astype(F32) for k, g in zip(kept, jnp.split(got, 2, axis=dimension)))
    return own, lax.ppermute(other.astype(BF16), "dp", in_pairs(2))


def piece_of(part, dimension, place):
    size = part.shape[dimension] // 4
    return lax.dynamic_slice_in_dim(part, place * size, size, dimension)


def add_rows(value, count):
    if count != 4:
        return lax.psum(value, "dp")
    one, two, three = (lax.ppermute(value, "dp", in_pairs(step)) for step in (1, 2, 3))
    return value, one, two, three


def turned(value):
    return pltpu.roll(value, HEAD_DIM // 2, 1)


def cosine_sine(table):
    lanes = lax.broadcasted_iota(jnp.int32, table.shape, 1)
    front, swapped = lanes < HEAD_DIM // 2, turned(table)
    return jnp.where(front, table, swapped), jnp.where(front, -swapped, table)


def scale_of(sums, at, width):
    return lax.rsqrt(sums[:, at : at + 1] * (1.0 / width) + norm_eps)


def window_of(b, block, back):
    first = jnp.maximum(b - back, 0)
    return first, pl.ds(pl.multiple_of(first * block, block), (back + 1) * block)


def allowed_in(docs, ahead, block, back):
    docs_row, docs_col = docs[:1, :], docs[:, :block].T[:, 1:2]
    window = (back + 1) * block
    rows = lax.broadcasted_iota(jnp.int32, (block, window), 0) + ahead * block
    columns = lax.broadcasted_iota(jnp.int32, (block, window), 1)
    return (docs_col == docs_row) & (columns <= rows)


def put_in_row(groups, row):
    block = row.shape[1]
    if len(groups) == 1:
        for at in range(row.shape[0]):
            row[at] = groups[0][at * block : (at + 1) * block, :]
        return
    near, beside, last = groups
    places = (beside, 0), (beside, 1), (near, 0), (last, 0), (beside, 2), (beside, 3), (near, 1), (last, 1)
    for at, (group, place) in enumerate(places):
        row[at] = group[place * block : (place + 1) * block, :]


def attend_kernel(
    shape,
    count,
    order,
    *refs,
):
    raws, refs = refs[:count], refs[count:]
    attend_body(shape, order, raws, *refs)


def attend_body(
    shape,
    order,
    raws,
    sums,
    gains,
    table,
    docs,
    attended,
    query,
    key,
    value,
    logsum,
    keys,
    values,
    raw,
):
    blocks, block, width, local, back, scale = shape
    heads = local // HEAD_DIM
    b = pl.program_id(0)

    @pl.when(b == 0)
    def _():
        put_in_row(raws, raw)
        keys[...] = jnp.zeros(keys.shape, BF16)
        values[...] = jnp.zeros(values.shape, BF16)

    total = sums[0].T
    cos, sin = cosine_sine(table[...])
    for which in range(2):
        inverse = scale_of(total, which, width)
        for h in range(heads):
            lanes = slice(h * HEAD_DIM, (h + 1) * HEAD_DIM)
            own = slice(which * local + h * HEAD_DIM, which * local + (h + 1) * HEAD_DIM)
            v = raw[order[b], :, own] * inverse * gains[which : which + 1, lanes]
            (query, key)[which][:, lanes] = (v * cos + turned(v) * sin).astype(BF16)
    value[...] = raw[order[b], :, 2 * local :].astype(BF16)
    now = pl.ds(pl.multiple_of(b * block, block), block)
    keys[now, :] = key[...]
    values[now, :] = value[...]
    first, window = window_of(b, block, back)
    allowed = allowed_in(docs[0], b - first, block, back)
    logsums = []
    for h in range(heads):
        lanes = slice(h * HEAD_DIM, (h + 1) * HEAD_DIM)
        scores = times_transposed(query[:, lanes], keys[window, lanes]) * scale
        scores = jnp.where(allowed, scores, -1e30)
        top = jnp.max(scores, axis=1, keepdims=True)
        weights = jnp.exp(scores - top)
        mass = jnp.sum(weights, axis=1, keepdims=True)
        shares = (weights * (1.0 / mass)).astype(BF16)
        attended[0, :, lanes] = times(shares, values[window, lanes]).astype(BF16)
        logsums.append(top + jnp.log(mass))
    logsum[0] = jnp.concatenate(logsums, axis=1).T


def attend_back_kernel(
    shape,
    order,
    raw,
    sums,
    gains,
    table,
    docs,
    query,
    keys,
    values,
    logsum,
    *refs,
):
    grads = refs[:-8]
    inner, grad_value, products, gain_parts, grad_query_sum, grad_key_sum, grad_value_sum, grad = refs[-8:]
    blocks, block, width, local, back, scale = shape
    heads = local // HEAD_DIM
    b = pl.program_id(0)

    @pl.when(b == 0)
    def _():
        put_in_row(grads, grad)
        grad_key_sum[...] = jnp.zeros(grad_key_sum.shape, F32)
        grad_value_sum[...] = jnp.zeros(grad_value_sum.shape, F32)
        gain_parts[...] = jnp.zeros(gain_parts.shape, F32)

    @pl.when(b < blocks)
    def _():
        first, window = window_of(b, block, back)
        allowed = allowed_in(docs[0], b - first, block, back)
        now = pl.ds(pl.multiple_of(b * block, block), block)
        tops = logsum[0].T
        for h in range(heads):
            lanes = slice(h * HEAD_DIM, (h + 1) * HEAD_DIM)
            q, k, v, g = query[:, lanes], keys[window, lanes], values[window, lanes], grad[order[b], :, lanes]
            scores = times_transposed(q, k) * scale
            chances = jnp.exp(jnp.where(allowed, scores, -1e30) - tops[:, h : h + 1])
            grad_shares = times_transposed(g, v)
            offset = jnp.sum(chances * grad_shares, axis=1, keepdims=True)
            grad_scores = (chances * (grad_shares - offset)).astype(BF16)
            grad_query_sum[now, lanes] = times(grad_scores, k) * scale
            grad_key_sum[window, lanes] += contract_rows(grad_scores, q) * scale
            grad_value_sum[window, lanes] += contract_rows(chances.astype(BF16), g)

    @pl.when(b >= back)
    def _():
        rows = pl.ds(pl.multiple_of((b - back) * block, block), block)
        total = sums[0].T
        cos, sin = cosine_sine(table[...])
        grad_value[0] = grad_value_sum[rows, :].astype(BF16)
        all_dots = []
        for which in range(2):
            inverse = scale_of(total, which, width)
            dots = jnp.zeros((block, 1), F32)
            for h in range(heads):
                lanes = slice(h * HEAD_DIM, (h + 1) * HEAD_DIM)
                own = slice(which * local + h * HEAD_DIM, which * local + (h + 1) * HEAD_DIM)
                unit = raw[0, :, own] * inverse
                g = (grad_query_sum, grad_key_sum)[which][rows, lanes]
                g = g * cos + turned(g * sin)
                gain_parts[which : which + 1, lanes] += jnp.sum(g * unit, axis=0, keepdims=True)
                c = g * gains[which : which + 1, lanes]
                inner[0, :, own] = c
                dots = dots + jnp.sum(c * unit, axis=1, keepdims=True)
            all_dots.append(dots)
        products[0] = jnp.concatenate(all_dots, axis=1).T


def attend(shape, order, raws, sums, gains, table, docs):
    blocks, block, width, local, back, scale = shape
    heads, length = local // HEAD_DIM, blocks * block
    in_row = lambda columns: pl.BlockSpec((block, columns), lambda b, order: (b, 0))
    arrived = lambda columns: pl.BlockSpec((1, block, columns), lambda b, order: (order[b], 0, 0))
    return pl.pallas_call(
        functools.partial(attend_kernel, shape, len(raws)),
        out_shape=(
            jax.ShapeDtypeStruct((blocks, block, local), BF16),
            jax.ShapeDtypeStruct((length, local), BF16),
            jax.ShapeDtypeStruct((length, local), BF16),
            jax.ShapeDtypeStruct((length, local), BF16),
            jax.ShapeDtypeStruct((blocks, heads, block), F32),
        ),
        grid_spec=pltpu.PrefetchScalarGridSpec(
            num_scalar_prefetch=1,
            grid=(blocks,),
            in_specs=[pl.BlockSpec(raw.shape, lambda b, order: (0, 0)) for raw in raws]
            + [
                pl.BlockSpec((1, 2, block), lambda b, order: (b, 0, 0)),
                pl.BlockSpec((2, local), lambda b, order: (0, 0)),
                in_row(HEAD_DIM),
                pl.BlockSpec((1, 2, (back + 1) * block), lambda b, order: (b, 0, 0)),
            ],
            out_specs=(
                arrived(local),
                in_row(local),
                in_row(local),
                in_row(local),
                pl.BlockSpec((1, heads, block), lambda b, order: (b, 0, 0)),
            ),
            scratch_shapes=[pltpu.VMEM((length, local), BF16)] * 2 + [pltpu.VMEM((blocks, block, 3 * local), F32)],
        ),
        compiler_params=pltpu.CompilerParams(vmem_limit_bytes=30 * 2**20),
        cost_estimate=pl.CostEstimate(flops=4 * 10**9, bytes_accessed=10**7, transcendentals=2 * 10**6),
    )(order, *raws, sums, gains, table, docs)


def attend_back(shape, order, raw, sums, gains, table, docs, query, key, value, logsum, grads):
    blocks, block, width, local, back, scale = shape
    heads, length = local // HEAD_DIM, blocks * block
    now = lambda b: jnp.minimum(b, blocks - 1)
    done = lambda b: jnp.maximum(b - back, 0)
    whole = pl.BlockSpec((length, local), lambda b, order: (0, 0))
    finished = lambda columns: pl.BlockSpec((1, block, columns), lambda b, order: (order[done(b)], 0, 0))
    return pl.pallas_call(
        functools.partial(attend_back_kernel, shape),
        out_shape=(
            jax.ShapeDtypeStruct((blocks, block, 2 * local), F32),
            jax.ShapeDtypeStruct((blocks, block, local), BF16),
            jax.ShapeDtypeStruct((blocks, 2, block), F32),
            jax.ShapeDtypeStruct((2, local), F32),
        ),
        grid_spec=pltpu.PrefetchScalarGridSpec(
            num_scalar_prefetch=1,
            grid=(blocks + back,),
            in_specs=[
                finished(3 * local),
                pl.BlockSpec((1, 2, block), lambda b, order: (done(b), 0, 0)),
                pl.BlockSpec((2, local), lambda b, order: (0, 0)),
                pl.BlockSpec((block, HEAD_DIM), lambda b, order: (done(b), 0)),
                pl.BlockSpec((1, 2, (back + 1) * block), lambda b, order: (now(b), 0, 0)),
                pl.BlockSpec((block, local), lambda b, order: (now(b), 0)),
                whole,
                whole,
                pl.BlockSpec((1, heads, block), lambda b, order: (now(b), 0, 0)),
            ]
            + [pl.BlockSpec(grad.shape, lambda b, order: (0, 0)) for grad in grads],
            out_specs=(
                finished(2 * local),
                finished(local),
                pl.BlockSpec((1, 2, block), lambda b, order: (done(b), 0, 0)),
                pl.BlockSpec((2, local), lambda b, order: (0, 0)),
            ),
            scratch_shapes=[pltpu.VMEM((length, local), F32)] * 3 + [pltpu.VMEM((blocks, block, local), BF16)],
        ),
        compiler_params=pltpu.CompilerParams(vmem_limit_bytes=28 * 2**20),
        cost_estimate=pl.CostEstimate(flops=8 * 10**9, bytes_accessed=2 * 10**7, transcendentals=2 * 10**6),
    )(order, raw, sums, gains, table, docs, query, key, value, logsum, *grads)


TILE = 256


def gated_grad(grad_act, gate, up):
    sigma = jax.nn.sigmoid(gate)
    grad_gate = grad_act * up * sigma * (1.0 + gate * (1.0 - sigma))
    return grad_gate.astype(BF16), (grad_act * gate * sigma).astype(BF16)


def feed_back_kernel(count, with_activated, *refs):
    grads, (weight, both) = refs[:count], refs[count : count + 2]
    *_, mine, others, rows = refs
    activated = refs[-4] if with_activated else None
    block, tile = grads[0].shape[0], weight.shape[0]
    units, half = mine.shape[-1] // 2, rows.shape[0] // 2
    j = pl.program_id(0)

    @pl.when(j == 0)
    def _():
        for at, grad in enumerate(grads):
            rows[at * block : (at + 1) * block, :] = grad[...]

    start = pl.multiple_of(j * tile, tile)
    gate, up = (both[:, pl.ds(at, tile)].astype(F32) for at in (start, start + units))
    if activated is not None:
        activated[...] = (gate * jax.nn.sigmoid(gate) * up).astype(BF16)
    grad_act = times_transposed(rows[...], weight[...])
    for at, part in zip((start, start + units), gated_grad(grad_act, gate, up)):
        for out, own in ((mine, part[:half]), (others, part[half:])):
            out[:, :, pl.ds(at, tile)] = own.reshape(out.shape[:2] + (tile,))


def feed_back(grads, down_weight, both, slot, slots, before=(), with_activated=False, limit=None):
    count, width = len(grads), grads[0].shape[1]
    units, tile = down_weight.shape[0], min(TILE, down_weight.shape[0])
    tiles, rows = units // tile, sum(grad.shape[0] for grad in grads)
    once = lambda shape: pl.BlockSpec(shape, lambda j: (0, 0), pipeline_mode=pl.Buffered(1))
    in_specs = [once(grad.shape) for grad in grads]
    in_specs += [pl.BlockSpec((tile, width), lambda j: (j, 0)), once(both.shape)]
    in_specs += [pl.BlockSpec(memory_space=pl.ANY)] * len(before)
    args = [*grads, down_weight, both, *before]
    part = rows // (2 * slots)
    extra_shape, extra_spec = (), ()
    if with_activated:
        extra_shape = (jax.ShapeDtypeStruct((rows, units), BF16),)
        extra_spec = (pl.BlockSpec((rows, tile), lambda j: (0, j)),)
    return pl.pallas_call(
        functools.partial(feed_back_kernel, count, with_activated),
        grid=(tiles,),
        out_shape=extra_shape + (jax.ShapeDtypeStruct((4, part, 2 * units), BF16),) * 2,
        in_specs=in_specs,
        out_specs=extra_spec + (pl.BlockSpec((slots, part, 2 * units), lambda j: (slot // slots, 0, 0)),) * 2,
        scratch_shapes=[pltpu.VMEM((rows, width), BF16)],
        input_output_aliases={count + 2 + at: at for at in range(len(before))},
        compiler_params=pltpu.CompilerParams(vmem_limit_bytes=(limit or 8 + 7 * rows // 192) * 2**20),
        cost_estimate=pl.CostEstimate(
            flops=2 * rows * width * units,
            bytes_accessed=2 * units * width + 12 * rows * units + 2 * rows * width,
            transcendentals=rows * units,
        ),
    )(*args)


def pieces_kernel(plan, count, place, *refs):
    sources, outs, sems = refs[:count], refs[count:-1], refs[-1]
    copies = []
    for out, parts in zip(outs, plan):
        size = out.shape[1]
        columns = pl.ds(pl.multiple_of(place[0] * size, size), size)
        at = 0
        for source, start, rows in parts:
            copies.append(
                pltpu.make_async_copy(
                    sources[source].at[pl.ds(start, rows), columns],
                    out.at[pl.ds(at, rows), :],
                    sems.at[len(copies)],
                )
            )
            at += rows
    for copy in copies:
        copy.start()
    for copy in copies:
        copy.wait()


def pieces_of(sources, plan, place, count=4):
    size = sources[0].shape[1] // count
    shapes = [(sum(rows for _, _, rows in parts), size) for parts in plan]
    return pl.pallas_call(
        functools.partial(pieces_kernel, plan, len(sources)),
        out_shape=[jax.ShapeDtypeStruct(shape, BF16) for shape in shapes],
        in_specs=[pl.BlockSpec(memory_space=pltpu.SMEM)] + [pl.BlockSpec(memory_space=pltpu.HBM)] * len(sources),
        out_specs=[pl.BlockSpec(memory_space=pltpu.HBM)] * len(plan),
        scratch_shapes=[pltpu.SemaphoreType.DMA((sum(len(parts) for parts in plan),))],
        compiler_params=pltpu.CompilerParams(vmem_limit_bytes=2**20),
        cost_estimate=pl.CostEstimate(
            flops=0, bytes_accessed=sum(4 * rows * columns for rows, columns in shapes), transcendentals=0
        ),
    )(jnp.reshape(place, (1,)).astype(jnp.int32), *sources)


def joined_rows(blocks):
    return pieces_of(blocks, [[(at, 0, block.shape[0]) for at, block in enumerate(blocks)]], 0, 1)[0]


def body(
    sizes,
    hidden_in,
    doc_ids,
    query_weight,
    key_weight,
    value_weight,
    output_weight,
    gate_weight,
    up_weight,
    down_weight,
    query_gain,
    key_gain,
    attention_gain,
    feedforward_gain,
    out_grad,
):
    tensor, rows = sizes["tensor"], sizes["dp"]
    moves = PairedCores() if tensor == 8 else AnyDevices(tensor)
    width = hidden_in.shape[1]
    local = query_weight.shape[1]
    hidden_units = gate_weight.shape[1]
    documents = doc_ids[0]
    length = documents.shape[0]
    block = length // tensor
    most = length // 4
    back = -(-(most - 1) // block)
    shape = (tensor, block, width, local, back, HEAD_DIM ** (-0.5))

    places = moves.order()
    steps = jnp.arange(tensor, dtype=jnp.int32)
    meets = places[None, :] == steps[:, None]
    order = jnp.sum(jnp.where(meets, steps[None, :], 0), axis=1)

    def in_row(value):
        parts = value.reshape(1, 2, tensor, block)
        return jnp.sum(jnp.where(meets[:, None, :, None], parts, 0.0), axis=2)

    def as_arrived(value):
        parts = value.transpose(1, 0, 2)[:, :, None]
        return jnp.sum(jnp.where(meets[None, :, :, None], parts, 0.0), axis=1).reshape(2, length)

    table = rope_table(length, HEAD_DIM)
    firsts = [max(b - back, 0) * block for b in range(tensor)]
    numbers = documents.astype(F32)
    docs = jnp.stack([numbers[first : first + (back + 1) * block] for first in firsts])
    own_docs = jnp.pad(numbers.reshape(tensor, block), ((0, 0), (0, back * block)))
    docs = jnp.stack([docs, own_docs], axis=1)
    gains = jnp.stack([query_gain, key_gain])

    def row_of(groups):
        return jnp.concatenate(moves.whole(groups), axis=0)

    def joined(group):
        return jnp.concatenate(group, axis=0)

    weight_qkv = jnp.concatenate([query_weight, key_weight, value_weight], axis=1)
    weight_gate_up = jnp.concatenate([gate_weight, up_weight], axis=1)
    paired = rows == 4 and tensor == 8

    def halves_of(whole):
        return jnp.split(whole, 2)

    def raw_of(*groups):
        return [times(joined(group), weight_qkv) for group in groups]

    hidden_groups, _, raw = moves.gather(hidden_in, early=raw_of)
    raw = raw + raw_of(hidden_groups[-1])
    squares = jnp.stack(
        [
            row_of([jnp.sum(jnp.square(part[:, at : at + local]), axis=1) for part in raw])
            for at in (0, local)
        ]
    )
    raws, raw = raw, row_of(raw)
    sums = moves.add(in_row(squares))
    tables = (sums, gains, table, docs)
    attended_blocks, query, key, value, logsum = attend(shape, order, raws, *tables)
    attended = attended_blocks.reshape(length, local)
    def join_hidden(passing):
        groups, _ = lax.optimization_barrier((hidden_groups, passing))
        return joined_rows(moves.whole(groups))

    attn_proj, _, hidden_all = moves.scatter(
        halves_of(attended),
        lambda part: times(part, output_weight),
        late=join_hidden if tensor == 8 else None,
    )
    if tensor != 8:
        hidden_all = hidden_groups[0][0]
    attn_scale = lax.rsqrt(jnp.mean(attn_proj * attn_proj, axis=1, keepdims=True) + norm_eps)
    attn_unit = attn_proj * attn_scale
    middle = hidden_in.astype(F32) + attn_unit * attention_gain
    middle_low = middle.astype(BF16)

    def activate(both):
        gate, up = both[:, :hidden_units], both[:, hidden_units:]
        return (gate * jax.nn.sigmoid(gate) * up).astype(BF16)

    def both_of(*groups):
        both = [times(joined(group), weight_gate_up) for group in groups]
        return both, [activate(part) for part in both]

    def to_pair(value):
        return lax.ppermute(value, "dp", in_pairs(2))

    def gather_pair(value):
        return lax.all_gather(value, "tensor", axis=0, tiled=True)

    pair_middle = to_pair(middle_low) if paired else None

    def both_early(*groups):
        return both_of(*groups), pair_middle

    middle_groups, _, made = moves.gather(middle_low, early=both_early)
    made, pair_middle = made or (([], []), None)
    if paired:
        pair_middle_all = gather_pair(pair_middle)
    both_groups, activated = (early + late for early, late in zip(made, both_of(middle_groups[-1])))
    activated = lax.optimization_barrier(row_of(activated))
    mlp_proj, _, _ = moves.scatter(halves_of(activated), lambda part: times(part, down_weight))
    mlp_scale = lax.rsqrt(jnp.mean(mlp_proj * mlp_proj, axis=1, keepdims=True) + norm_eps)
    mlp_unit = mlp_proj * mlp_scale
    result = middle + mlp_unit * feedforward_gain

    grad_out = out_grad.astype(F32)
    grad_mlp = norm_back(grad_out, mlp_unit, mlp_scale, feedforward_gain).astype(BF16)
    feedforward_part = jnp.sum(grad_out * mlp_unit, axis=0)
    pair_both = None
    if paired:
        pair_middle_all, grad_mlp = lax.optimization_barrier((pair_middle_all, grad_mlp))
        pair_both = times(pair_middle_all, weight_gate_up).astype(BF16)

    def back_early(near, beside):
        part = feed_back(near, down_weight, both_groups[0], 2, 1)
        part = feed_back(beside, down_weight, both_groups[1], 0, 2, part)
        return part, pair_grad_mlp[1]

    pair_grad_mlp = [None, None]
    if paired:
        first_half, second_half = jnp.split(grad_mlp, 2, axis=1)
        first_half, second_half = lax.optimization_barrier((to_pair(first_half), second_half))
        pair_grad_mlp = [first_half, to_pair(second_half)]
    meanwhile = (pair_both, pair_grad_mlp[0])
    grad_mlp_groups, (pair_both, first_half), made = moves.gather(grad_mlp, meanwhile, back_early)
    if tensor == 8:
        made, second_half = made
        grad_gate_up = feed_back(grad_mlp_groups[-1], down_weight, both_groups[2], 3, 1, made, limit=60)
        grad_gate_up = [half.reshape(length // 2, 2 * hidden_units) for half in grad_gate_up]
    else:
        grad_act = times_transposed(grad_mlp_groups[0][0], down_weight)
        both = both_groups[0].astype(F32)
        grad_gate_up = gated_grad(grad_act, both[:, :hidden_units], both[:, hidden_units:])
        grad_gate_up = halves_of(jnp.concatenate(grad_gate_up, axis=1))
    if paired:
        pair_grad_mlp_all = gather_pair(jnp.concatenate([first_half, second_half], axis=1))

    me = lax.axis_index("dp")
    half_rows = length // 2

    def own_weight_pieces(place):
        blocks = moves.whole(middle_groups) + moves.whole(grad_mlp_groups)
        part = [(at, 0, block) for at in range(16)]
        mine, others, grads = pieces_of(blocks, [part[:4], part[4:8], part[8:]], place)
        return [
            contract_rows(grads, activated),
            contract_rows(mine, grad_gate_up[0]) + contract_rows(others, grad_gate_up[1]),
        ]

    def pair_weight_pieces(place):
        plan = [[(0, 0, half_rows)], [(0, half_rows, half_rows)], [(1, 0, length)]]
        first, second, grads = pieces_of([pair_middle_all, pair_grad_mlp_all], plan, place)
        return [
            contract_rows(grads, pair_activated),
            contract_rows(first, pair_gate_up[0]) + contract_rows(second, pair_gate_up[1]),
        ]

    def gate_up_own(place):
        part = [(at, 0, block) for at in range(8)]
        mine, others = pieces_of(moves.whole(middle_groups), [part[:4], part[4:]], place)
        return contract_rows(mine, grad_gate_up[0]) + contract_rows(others, grad_gate_up[1])

    def gate_up_pair(place):
        plan = [[(0, 0, half_rows)], [(0, half_rows, half_rows)]]
        first, second = pieces_of([pair_middle_all], plan, place)
        return contract_rows(first, pair_gate_up[0]) + contract_rows(second, pair_gate_up[1])

    def down_pieces(place):
        part = [(at, 0, block) for at in range(8)]
        blocks = moves.whole(grad_mlp_groups) + [pair_grad_mlp_all]
        own, pair = pieces_of(blocks, [part, [(8, 0, length)]], place)
        return contract_rows(own, activated) + contract_rows(pair, pair_activated)

    def own_away(sent):
        nonlocal grad_mlp_groups, middle_groups
        grad_mlp_groups, middle_groups, _ = lax.optimization_barrier((grad_mlp_groups, middle_groups, sent))
        return own_weight_pieces(me ^ 1)

    def pair_back(passing):
        grads, _ = lax.optimization_barrier((pair_grad_mlp_all, passing))
        pair_activated, *pair_gate_up = feed_back([grads], down_weight, pair_both, 0, 4, with_activated=True)
        return pair_activated, [half.reshape(half_rows, 2 * hidden_units) for half in pair_gate_up]

    back_part, away, pair_gate_up = moves.scatter(
        grad_gate_up,
        lambda part: times_transposed(part, weight_gate_up),
        own_away if paired else None,
        pair_back if paired else None,
    )
    grad_middle = grad_out + back_part

    grad_proj = norm_back(grad_middle, attn_unit, attn_scale, attention_gain).astype(BF16)
    attention_part = jnp.sum(grad_middle * attn_unit, axis=0)
    if paired:
        (pair_activated, pair_gate_up), grad_proj = lax.optimization_barrier((pair_gate_up, grad_proj))
        away = [(own + pair).astype(BF16) for own, pair in zip(away, pair_weight_pieces(me ^ 1))]
        away = [away[0], *jnp.split(away[1], 2, axis=1)]
        away = [half for part in away for half in jnp.split(part, 2)]
        got = [lax.ppermute(part, "dp", in_pairs(1)) for part in away]

    def attended_early(*groups):
        return [times_transposed(joined(group), output_weight).astype(BF16) for group in groups]

    def proj_early(*groups):
        if not paired:
            return attended_early(*groups), None
        return attended_early(*groups), gate_up_own(me)

    grad_proj_groups, away, made = moves.gather(grad_proj, away, proj_early)
    made, *rest = made or ([],)
    if paired:
        (kept_gate_up,) = rest
    else:
        down_grad = scatter_rows(contract_rows(activated, row_of(grad_mlp_groups)).astype(BF16), 1).astype(F32)
        back = contract_rows(row_of(middle_groups), jnp.concatenate(grad_gate_up, axis=0))
        gate_grad, up_grad = jnp.split(scatter_rows(back.astype(BF16), 0).astype(F32), 2, axis=1)
    grad_attended = made + attended_early(grad_proj_groups[-1])
    raw_blocks = raw.reshape(tensor, block, 3 * local)
    inner, grad_value, products, gain_parts = attend_back(
        shape, order, raw_blocks, *tables, query, key, value, logsum, grad_attended
    )
    if paired:
        (products, grad_proj_groups), *got[:2] = lax.optimization_barrier(
            ((products, grad_proj_groups), *got[:2])
        )
    output_part = sum(
        contract_rows(joined(right), left) for left, right in zip(moves.groups(attended), grad_proj_groups)
    )
    place = lax.axis_index("tensor") * local
    spread = lax.dynamic_update_slice(jnp.zeros((2, width), F32), gain_parts, (0, place))
    spread = jnp.concatenate([spread, attention_part[None], feedforward_part[None]], axis=0)
    packed = moves.add(jnp.concatenate([products.reshape(-1), spread.reshape(-1)]).reshape(-1, 256))
    if paired:
        packed, got[2] = lax.optimization_barrier((packed, got[2]))
    packed = packed.reshape(-1)
    products = as_arrived(packed[: 2 * length].reshape(tensor, 2, block)).T * (1.0 / width)
    gain_sums = add_rows(packed[2 * length :], rows)
    inner = inner.reshape(length, 2 * local)
    grad_qkv = [None, None, grad_value.reshape(length, local)]
    flat = as_arrived(sums).T
    for which in range(2):
        own = slice(which * local, (which + 1) * local)
        inverse = lax.rsqrt(flat[:, which : which + 1] * (1.0 / width) + norm_eps)
        unit = raw[:, own] * inverse
        grad_qkv[which] = (inverse * (inner[:, own] - unit * products[:, which : which + 1])).astype(BF16)
    grad_qkv = jnp.concatenate(grad_qkv, axis=1)
    qkv_part = contract_rows(hidden_all, grad_qkv).astype(BF16)
    projections_part = jnp.concatenate([qkv_part, output_part.astype(BF16)], axis=1)
    if paired:
        projections_part, *got[3:5] = lax.optimization_barrier((projections_part, *got[3:5]))
    grad_qkv, projections_part = lax.optimization_barrier((grad_qkv, projections_part))
    projections_grad = scatter_rows(projections_part, 0)

    def finish_gate(sent):
        nonlocal pair_middle_all, pair_gate_up
        values, _ = lax.optimization_barrier(((pair_middle_all, pair_gate_up), sent))
        pair_middle_all, pair_gate_up = values
        kept = kept_gate_up + gate_up_pair(me)
        gate_got = jnp.concatenate(got[2:4], axis=0).astype(F32)
        return kept[:, :hidden_units] + gate_got, kept[:, hidden_units:]

    def finish_down(passing):
        nonlocal grad_mlp_groups, pair_grad_mlp_all
        values, _ = lax.optimization_barrier(((grad_mlp_groups, pair_grad_mlp_all), passing))
        grad_mlp_groups, pair_grad_mlp_all = values
        return (down_pieces(me) + jnp.concatenate(got[:2], axis=0).astype(F32)).T

    input_part, made, down_made = moves.scatter(
        halves_of(grad_qkv),
        lambda part: times_transposed(part, weight_qkv),
        finish_gate if paired else None,
        finish_down if paired else None,
    )
    input_grad = grad_middle + input_part
    if paired:
        (gate_grad, up_kept), down_grad = made, down_made
        up_grad = up_kept + jnp.concatenate(got[4:], axis=0).astype(F32)
        results = input_grad, down_grad, gate_grad, up_grad
        gain_sums, results = lax.optimization_barrier((gain_sums, results))
        input_grad, down_grad, gate_grad, up_grad = results
        own, one, two, three = gain_sums
        gain_sums = (own + one) + (two + three)
    query_grad, key_grad, value_grad, output_grad = (
        projections_grad[:, at * local : (at + 1) * local].astype(F32) for at in range(4)
    )
    output_grad = output_grad.T
    summed = gain_sums.reshape(4, width)
    return (
        result,
        input_grad,
        query_grad,
        key_grad,
        value_grad,
        output_grad,
        gate_grad,
        up_grad,
        down_grad,
        summed[0],
        summed[1],
        summed[2],
        summed[3],
    )


def solution(mesh):
    in_specs = (
        P(("dp", "tensor"), None),
        P("dp", None),
        P(None, "tensor"),
        P(None, "tensor"),
        P(None, "tensor"),
        P("tensor", None),
        P(None, "tensor"),
        P(None, "tensor"),
        P("tensor", None),
        P("tensor"),
        P("tensor"),
        P(),
        P(),
        P(("dp", "tensor"), None),
    )
    out_specs = (
        P(("dp", "tensor"), None),
        P(("dp", "tensor"), None),
        P("dp", "tensor"),
        P("dp", "tensor"),
        P("dp", "tensor"),
        P("tensor", "dp"),
        P("dp", "tensor"),
        P("dp", "tensor"),
        P("tensor", "dp"),
        P(),
        P(),
        P(),
        P(),
    )
    sizes = {axis: mesh.shape[axis] for axis in ("dp", "tensor")}
    return jax.shard_map(
        functools.partial(body, sizes), mesh=mesh, in_specs=in_specs, out_specs=out_specs, check_vma=False
    )
```

```python
import functools

import jax
import jax.numpy as jnp
from jax import lax
from jax.experimental import pallas as pl
from jax.experimental.pallas import tpu as pltpu
from jax.sharding import PartitionSpec as P

HEAD_DIM = 128
BF16 = jnp.bfloat16
F32 = jnp.float32

norm_eps = 1e-06
rope_base = 500000.0


def contract_rows(left, right):
    return lax.dot_general(left, right, (((0,), (0,)), ((), ())), preferred_element_type=F32)


def times_transposed(left, right):
    return lax.dot_general(left, right, (((1,), (1,)), ((), ())), preferred_element_type=F32)


def times(left, right):
    return jnp.dot(left, right, preferred_element_type=F32)


def rope_table(length, head_dim):
    half = head_dim // 2
    freq = rope_base ** (-(2.0 * jnp.arange(half, dtype=F32)) / head_dim)
    angle = jnp.arange(length, dtype=F32)[:, None] * freq[None, :]
    return jnp.concatenate([jnp.cos(angle), jnp.sin(angle)], axis=1)


def norm_back(grad, unit, inverse, gain):
    inner = grad * gain
    return inverse * (inner - unit * jnp.mean(inner * unit, axis=1, keepdims=True))


class PairedCores:
    def __init__(self):
        turn = lambda low, high: [(i, i ^ (low if i % 2 == 0 else high)) for i in range(8)]
        self.first, self.second, self.core = turn(2, 4), turn(4, 2), turn(1, 1)

    def send(self, value, way):
        return lax.ppermute(value, "tensor", way)

    def order(self):
        me = lax.axis_index("tensor")
        near = jnp.where(me % 2 == 0, 2, 4)
        far = 6 - near
        return jnp.stack([me ^ near, me ^ far, me, me ^ 6, me ^ 1 ^ far, me ^ 1 ^ near, me ^ 1, me ^ 7])

    def gather(self, own, meanwhile=None, early=None):
        first, second = self.send(own, self.first), self.send(own, self.second)
        other = self.send(own, self.core)
        if meanwhile is not None:
            second, meanwhile = lax.optimization_barrier((second, meanwhile))
        opposite = self.send(second, self.first)
        first_other, second_other = self.send(first, self.core), self.send(second, self.core)
        groups = [[own, other], [first, second, first_other, second_other]]
        made = None
        if early is not None:
            opposite, made = lax.optimization_barrier((opposite, early(*groups)))
        groups.append([opposite, self.send(opposite, self.core)])
        return groups, meanwhile, made

    def whole(self, groups):
        near, middle, last = groups
        if not isinstance(near, list):
            near, middle, last = jnp.split(near, 2), jnp.split(middle, 4), jnp.split(last, 2)
        first, second, first_other, second_other = middle
        return [first, second, near[0], last[0], first_other, second_other, near[1], last[1]]

    def groups(self, whole):
        first, second, own, opposite, first_other, second_other, other, opposite_other = jnp.split(whole, 8)
        groups = [[own, other], [first, second, first_other, second_other], [opposite, opposite_other]]
        return [jnp.concatenate(group, axis=0) for group in groups]

    def scatter(self, halves, product, meanwhile=None, late=None):
        mine, others = halves
        from_core = self.send(product(others).astype(BF16), self.core)
        own_part, from_core = lax.optimization_barrier((product(mine).astype(BF16), from_core))
        first, second, own, opposite = (
            part.astype(F32) + other.astype(F32)
            for part, other in zip(jnp.split(own_part, 4), jnp.split(from_core, 4))
        )
        sent = opposite.astype(BF16), first.astype(BF16)
        passing, from_first = (self.send(part, self.first) for part in sent)
        if meanwhile is not None:
            passing, meanwhile = lax.optimization_barrier((passing, meanwhile(sent)))
        from_second = self.send((second + passing.astype(F32)).astype(BF16), self.second)
        if late is not None:
            from_second, late = lax.optimization_barrier((from_second, late(passing)))
        return own + from_first.astype(F32) + from_second.astype(F32), meanwhile, late

    def add(self, value):
        for bit in (1, 2, 4):
            value = value + self.send(value, [(i, i ^ bit) for i in range(8)])
        return value


class AnyDevices:
    def __init__(self, size):
        self.size = size

    def order(self):
        return jnp.arange(self.size)

    def gather(self, own, meanwhile=None, early=None):
        return [[lax.all_gather(own, "tensor", axis=0, tiled=True)]], meanwhile, []

    def groups(self, whole):
        return [whole]

    def whole(self, groups):
        return groups[0] if isinstance(groups[0], list) else groups

    def scatter(self, halves, product, meanwhile=None, late=None):
        part = product(jnp.concatenate(halves, axis=0)).astype(BF16)
        total = lax.psum_scatter(part, "tensor", scatter_dimension=0, tiled=True).astype(F32)
        return total, meanwhile, late

    def add(self, value):
        return lax.psum(value, "tensor")


def in_pairs(step):
    return [(i, i ^ step) for i in range(4)]


def scatter_rows(part, dimension):
    return lax.psum_scatter(part, "dp", scatter_dimension=dimension, tiled=True)


def halve_rows(part, dimension):
    me = lax.axis_index("dp")
    away = [piece_of(part, dimension, me ^ step) for step in (1, 3)]
    kept = [piece_of(part, dimension, me ^ step) for step in (0, 2)]
    return kept, lax.ppermute(jnp.concatenate(away, axis=dimension), "dp", in_pairs(1))


def quarter_rows(halved, dimension):
    kept, got = halved
    own, other = (k.astype(F32) + g.astype(F32) for k, g in zip(kept, jnp.split(got, 2, axis=dimension)))
    return own, lax.ppermute(other.astype(BF16), "dp", in_pairs(2))


def piece_of(part, dimension, place):
    size = part.shape[dimension] // 4
    return lax.dynamic_slice_in_dim(part, place * size, size, dimension)


def add_rows(value, count):
    if count != 4:
        return lax.psum(value, "dp")
    one, two, three = (lax.ppermute(value, "dp", in_pairs(step)) for step in (1, 2, 3))
    return value, one, two, three


def turned(value):
    return pltpu.roll(value, HEAD_DIM // 2, 1)


def cosine_sine(table):
    lanes = lax.broadcasted_iota(jnp.int32, table.shape, 1)
    front, swapped = lanes < HEAD_DIM // 2, turned(table)
    return jnp.where(front, table, swapped), jnp.where(front, -swapped, table)


def scale_of(sums, at, width):
    return lax.rsqrt(sums[:, at : at + 1] * (1.0 / width) + norm_eps)


def window_of(b, block, back):
    first = jnp.maximum(b - back, 0)
    return first, pl.ds(pl.multiple_of(first * block, block), (back + 1) * block)


def allowed_in(docs, ahead, block, back):
    docs_row, docs_col = docs[:1, :], docs[:, :block].T[:, 1:2]
    window = (back + 1) * block
    rows = lax.broadcasted_iota(jnp.int32, (block, window), 0) + ahead * block
    columns = lax.broadcasted_iota(jnp.int32, (block, window), 1)
    return (docs_col == docs_row) & (columns <= rows)


def put_in_row(groups, row):
    block = row.shape[1]
    if len(groups) == 1:
        for at in range(row.shape[0]):
            row[at] = groups[0][at * block : (at + 1) * block, :]
        return
    near, beside, last = groups
    places = (beside, 0), (beside, 1), (near, 0), (last, 0), (beside, 2), (beside, 3), (near, 1), (last, 1)
    for at, (group, place) in enumerate(places):
        row[at] = group[place * block : (place + 1) * block, :]


def attend_kernel(
    shape,
    count,
    order,
    *refs,
):
    raws, refs = refs[:count], refs[count:]
    attend_body(shape, order, raws, *refs)


def attend_body(
    shape,
    order,
    raws,
    sums,
    gains,
    table,
    docs,
    attended,
    query,
    key,
    value,
    logsum,
    keys,
    values,
    raw,
):
    blocks, block, width, local, back, scale = shape
    heads = local // HEAD_DIM
    b = pl.program_id(0)

    @pl.when(b == 0)
    def _():
        put_in_row(raws, raw)
        keys[...] = jnp.zeros(keys.shape, BF16)
        values[...] = jnp.zeros(values.shape, BF16)

    total = sums[0].T
    cos, sin = cosine_sine(table[...])
    for which in range(2):
        inverse = scale_of(total, which, width)
        for h in range(heads):
            lanes = slice(h * HEAD_DIM, (h + 1) * HEAD_DIM)
            own = slice(which * local + h * HEAD_DIM, which * local + (h + 1) * HEAD_DIM)
            v = raw[order[b], :, own] * inverse * gains[which : which + 1, lanes]
            (query, key)[which][:, lanes] = (v * cos + turned(v) * sin).astype(BF16)
    value[...] = raw[order[b], :, 2 * local :].astype(BF16)
    now = pl.ds(pl.multiple_of(b * block, block), block)
    keys[now, :] = key[...]
    values[now, :] = value[...]
    first, window = window_of(b, block, back)
    allowed = allowed_in(docs[0], b - first, block, back)
    logsums = []
    for h in range(heads):
        lanes = slice(h * HEAD_DIM, (h + 1) * HEAD_DIM)
        scores = times_transposed(query[:, lanes], keys[window, lanes]) * scale
        scores = jnp.where(allowed, scores, -1e30)
        top = jnp.max(scores, axis=1, keepdims=True)
        weights = jnp.exp(scores - top)
        mass = jnp.sum(weights, axis=1, keepdims=True)
        shares = (weights * (1.0 / mass)).astype(BF16)
        attended[0, :, lanes] = times(shares, values[window, lanes]).astype(BF16)
        logsums.append(top + jnp.log(mass))
    logsum[0] = jnp.concatenate(logsums, axis=1).T


def attend_back_kernel(
    shape,
    order,
    raw,
    sums,
    gains,
    table,
    docs,
    query,
    keys,
    values,
    logsum,
    *refs,
):
    grads = refs[:-8]
    inner, grad_value, products, gain_parts, grad_query_sum, grad_key_sum, grad_value_sum, grad = refs[-8:]
    blocks, block, width, local, back, scale = shape
    heads = local // HEAD_DIM
    b = pl.program_id(0)

    @pl.when(b == 0)
    def _():
        put_in_row(grads, grad)
        grad_key_sum[...] = jnp.zeros(grad_key_sum.shape, F32)
        grad_value_sum[...] = jnp.zeros(grad_value_sum.shape, F32)
        gain_parts[...] = jnp.zeros(gain_parts.shape, F32)

    @pl.when(b < blocks)
    def _():
        first, window = window_of(b, block, back)
        allowed = allowed_in(docs[0], b - first, block, back)
        now = pl.ds(pl.multiple_of(b * block, block), block)
        tops = logsum[0].T
        for h in range(heads):
            lanes = slice(h * HEAD_DIM, (h + 1) * HEAD_DIM)
            q, k, v, g = query[:, lanes], keys[window, lanes], values[window, lanes], grad[order[b], :, lanes]
            scores = times_transposed(q, k) * scale
            chances = jnp.exp(jnp.where(allowed, scores, -1e30) - tops[:, h : h + 1])
            grad_shares = times_transposed(g, v)
            offset = jnp.sum(chances * grad_shares, axis=1, keepdims=True)
            grad_scores = (chances * (grad_shares - offset)).astype(BF16)
            grad_query_sum[now, lanes] = times(grad_scores, k) * scale
            grad_key_sum[window, lanes] += contract_rows(grad_scores, q) * scale
            grad_value_sum[window, lanes] += contract_rows(chances.astype(BF16), g)

    @pl.when(b >= back)
    def _():
        rows = pl.ds(pl.multiple_of((b - back) * block, block), block)
        total = sums[0].T
        cos, sin = cosine_sine(table[...])
        grad_value[0] = grad_value_sum[rows, :].astype(BF16)
        all_dots = []
        for which in range(2):
            inverse = scale_of(total, which, width)
            dots = jnp.zeros((block, 1), F32)
            for h in range(heads):
                lanes = slice(h * HEAD_DIM, (h + 1) * HEAD_DIM)
                own = slice(which * local + h * HEAD_DIM, which * local + (h + 1) * HEAD_DIM)
                unit = raw[0, :, own] * inverse
                g = (grad_query_sum, grad_key_sum)[which][rows, lanes]
                g = g * cos + turned(g * sin)
                gain_parts[which : which + 1, lanes] += jnp.sum(g * unit, axis=0, keepdims=True)
                c = g * gains[which : which + 1, lanes]
                inner[0, :, own] = c
                dots = dots + jnp.sum(c * unit, axis=1, keepdims=True)
            all_dots.append(dots)
        products[0] = jnp.concatenate(all_dots, axis=1).T


def attend(shape, order, raws, sums, gains, table, docs):
    blocks, block, width, local, back, scale = shape
    heads, length = local // HEAD_DIM, blocks * block
    in_row = lambda columns: pl.BlockSpec((block, columns), lambda b, order: (b, 0))
    arrived = lambda columns: pl.BlockSpec((1, block, columns), lambda b, order: (order[b], 0, 0))
    return pl.pallas_call(
        functools.partial(attend_kernel, shape, len(raws)),
        out_shape=(
            jax.ShapeDtypeStruct((blocks, block, local), BF16),
            jax.ShapeDtypeStruct((length, local), BF16),
            jax.ShapeDtypeStruct((length, local), BF16),
            jax.ShapeDtypeStruct((length, local), BF16),
            jax.ShapeDtypeStruct((blocks, heads, block), F32),
        ),
        grid_spec=pltpu.PrefetchScalarGridSpec(
            num_scalar_prefetch=1,
            grid=(blocks,),
            in_specs=[pl.BlockSpec(raw.shape, lambda b, order: (0, 0)) for raw in raws]
            + [
                pl.BlockSpec((1, 2, block), lambda b, order: (b, 0, 0)),
                pl.BlockSpec((2, local), lambda b, order: (0, 0)),
                in_row(HEAD_DIM),
                pl.BlockSpec((1, 2, (back + 1) * block), lambda b, order: (b, 0, 0)),
            ],
            out_specs=(
                arrived(local),
                in_row(local),
                in_row(local),
                in_row(local),
                pl.BlockSpec((1, heads, block), lambda b, order: (b, 0, 0)),
            ),
            scratch_shapes=[pltpu.VMEM((length, local), BF16)] * 2 + [pltpu.VMEM((blocks, block, 3 * local), F32)],
        ),
        compiler_params=pltpu.CompilerParams(vmem_limit_bytes=60 * 2**20),
        cost_estimate=pl.CostEstimate(flops=4 * 10**9, bytes_accessed=10**7, transcendentals=2 * 10**6),
    )(order, *raws, sums, gains, table, docs)


def attend_back(shape, order, raw, sums, gains, table, docs, query, key, value, logsum, grads):
    blocks, block, width, local, back, scale = shape
    heads, length = local // HEAD_DIM, blocks * block
    now = lambda b: jnp.minimum(b, blocks - 1)
    done = lambda b: jnp.maximum(b - back, 0)
    whole = pl.BlockSpec((length, local), lambda b, order: (0, 0))
    finished = lambda columns: pl.BlockSpec((1, block, columns), lambda b, order: (order[done(b)], 0, 0))
    return pl.pallas_call(
        functools.partial(attend_back_kernel, shape),
        out_shape=(
            jax.ShapeDtypeStruct((blocks, block, 2 * local), F32),
            jax.ShapeDtypeStruct((blocks, block, local), BF16),
            jax.ShapeDtypeStruct((blocks, 2, block), F32),
            jax.ShapeDtypeStruct((2, local), F32),
        ),
        grid_spec=pltpu.PrefetchScalarGridSpec(
            num_scalar_prefetch=1,
            grid=(blocks + back,),
            in_specs=[
                finished(3 * local),
                pl.BlockSpec((1, 2, block), lambda b, order: (done(b), 0, 0)),
                pl.BlockSpec((2, local), lambda b, order: (0, 0)),
                pl.BlockSpec((block, HEAD_DIM), lambda b, order: (done(b), 0)),
                pl.BlockSpec((1, 2, (back + 1) * block), lambda b, order: (now(b), 0, 0)),
                pl.BlockSpec((block, local), lambda b, order: (now(b), 0)),
                whole,
                whole,
                pl.BlockSpec((1, heads, block), lambda b, order: (now(b), 0, 0)),
            ]
            + [pl.BlockSpec(grad.shape, lambda b, order: (0, 0)) for grad in grads],
            out_specs=(
                finished(2 * local),
                finished(local),
                pl.BlockSpec((1, 2, block), lambda b, order: (done(b), 0, 0)),
                pl.BlockSpec((2, local), lambda b, order: (0, 0)),
            ),
            scratch_shapes=[pltpu.VMEM((length, local), F32)] * 3 + [pltpu.VMEM((blocks, block, local), BF16)],
        ),
        compiler_params=pltpu.CompilerParams(vmem_limit_bytes=28 * 2**20),
        cost_estimate=pl.CostEstimate(flops=8 * 10**9, bytes_accessed=2 * 10**7, transcendentals=2 * 10**6),
    )(order, raw, sums, gains, table, docs, query, key, value, logsum, *grads)


TILE = 256


def gated_grad(grad_act, gate, up):
    sigma = jax.nn.sigmoid(gate)
    grad_gate = grad_act * up * sigma * (1.0 + gate * (1.0 - sigma))
    return grad_gate.astype(BF16), (grad_act * gate * sigma).astype(BF16)


def feed_back_kernel(count, with_activated, *refs):
    grads, (weight, both) = refs[:count], refs[count : count + 2]
    *_, mine, others, rows = refs
    activated = refs[-4] if with_activated else None
    block, tile = grads[0].shape[0], weight.shape[0]
    units, half = mine.shape[-1] // 2, rows.shape[0] // 2
    j = pl.program_id(0)

    @pl.when(j == 0)
    def _():
        for at, grad in enumerate(grads):
            rows[at * block : (at + 1) * block, :] = grad[...]

    start = pl.multiple_of(j * tile, tile)
    gate, up = (both[:, pl.ds(at, tile)].astype(F32) for at in (start, start + units))
    if activated is not None:
        activated[...] = (gate * jax.nn.sigmoid(gate) * up).astype(BF16)
    grad_act = times_transposed(rows[...], weight[...])
    for at, part in zip((start, start + units), gated_grad(grad_act, gate, up)):
        for out, own in ((mine, part[:half]), (others, part[half:])):
            out[:, :, pl.ds(at, tile)] = own.reshape(out.shape[:2] + (tile,))


def feed_back(grads, down_weight, both, slot, slots, before=(), with_activated=False, limit=None):
    count, width = len(grads), grads[0].shape[1]
    units, tile = down_weight.shape[0], min(TILE, down_weight.shape[0])
    tiles, rows = units // tile, sum(grad.shape[0] for grad in grads)
    once = lambda shape: pl.BlockSpec(shape, lambda j: (0, 0), pipeline_mode=pl.Buffered(1))
    in_specs = [once(grad.shape) for grad in grads]
    in_specs += [pl.BlockSpec((tile, width), lambda j: (j, 0)), once(both.shape)]
    in_specs += [pl.BlockSpec(memory_space=pl.ANY)] * len(before)
    args = [*grads, down_weight, both, *before]
    part = rows // (2 * slots)
    extra_shape, extra_spec = (), ()
    if with_activated:
        extra_shape = (jax.ShapeDtypeStruct((rows, units), BF16),)
        extra_spec = (pl.BlockSpec((rows, tile), lambda j: (0, j)),)
    return pl.pallas_call(
        functools.partial(feed_back_kernel, count, with_activated),
        grid=(tiles,),
        out_shape=extra_shape + (jax.ShapeDtypeStruct((4, part, 2 * units), BF16),) * 2,
        in_specs=in_specs,
        out_specs=extra_spec + (pl.BlockSpec((slots, part, 2 * units), lambda j: (slot // slots, 0, 0)),) * 2,
        scratch_shapes=[pltpu.VMEM((rows, width), BF16)],
        input_output_aliases={count + 2 + at: at for at in range(len(before))},
        compiler_params=pltpu.CompilerParams(vmem_limit_bytes=(limit or 8 + 7 * rows // 192) * 2**20),
        cost_estimate=pl.CostEstimate(
            flops=2 * rows * width * units,
            bytes_accessed=2 * units * width + 12 * rows * units + 2 * rows * width,
            transcendentals=rows * units,
        ),
    )(*args)


def pieces_kernel(plan, count, place, *refs):
    sources, outs, sems = refs[:count], refs[count:-1], refs[-1]
    copies = []
    for out, parts in zip(outs, plan):
        size = out.shape[1]
        columns = pl.ds(pl.multiple_of(place[0] * size, size), size)
        at = 0
        for source, start, rows in parts:
            copies.append(
                pltpu.make_async_copy(
                    sources[source].at[pl.ds(start, rows), columns],
                    out.at[pl.ds(at, rows), :],
                    sems.at[len(copies)],
                )
            )
            at += rows
    for copy in copies:
        copy.start()
    for copy in copies:
        copy.wait()


def pieces_of(sources, plan, place, count=4):
    size = sources[0].shape[1] // count
    shapes = [(sum(rows for _, _, rows in parts), size) for parts in plan]
    return pl.pallas_call(
        functools.partial(pieces_kernel, plan, len(sources)),
        out_shape=[jax.ShapeDtypeStruct(shape, BF16) for shape in shapes],
        in_specs=[pl.BlockSpec(memory_space=pltpu.SMEM)] + [pl.BlockSpec(memory_space=pltpu.HBM)] * len(sources),
        out_specs=[pl.BlockSpec(memory_space=pltpu.HBM)] * len(plan),
        scratch_shapes=[pltpu.SemaphoreType.DMA((sum(len(parts) for parts in plan),))],
        compiler_params=pltpu.CompilerParams(vmem_limit_bytes=2**20),
        cost_estimate=pl.CostEstimate(
            flops=0, bytes_accessed=sum(4 * rows * columns for rows, columns in shapes), transcendentals=0
        ),
    )(jnp.reshape(place, (1,)).astype(jnp.int32), *sources)


def joined_rows(blocks):
    return pieces_of(blocks, [[(at, 0, block.shape[0]) for at, block in enumerate(blocks)]], 0, 1)[0]


def body(
    sizes,
    hidden_in,
    doc_ids,
    query_weight,
    key_weight,
    value_weight,
    output_weight,
    gate_weight,
    up_weight,
    down_weight,
    query_gain,
    key_gain,
    attention_gain,
    feedforward_gain,
    out_grad,
):
    tensor, rows = sizes["tensor"], sizes["dp"]
    moves = PairedCores() if tensor == 8 else AnyDevices(tensor)
    width = hidden_in.shape[1]
    local = query_weight.shape[1]
    hidden_units = gate_weight.shape[1]
    documents = doc_ids[0]
    length = documents.shape[0]
    block = length // tensor
    most = length // 4
    back = -(-(most - 1) // block)
    shape = (tensor, block, width, local, back, HEAD_DIM ** (-0.5))

    places = moves.order()
    steps = jnp.arange(tensor, dtype=jnp.int32)
    meets = places[None, :] == steps[:, None]
    order = jnp.sum(jnp.where(meets, steps[None, :], 0), axis=1)

    def in_row(value):
        parts = value.reshape(1, 2, tensor, block)
        return jnp.sum(jnp.where(meets[:, None, :, None], parts, 0.0), axis=2)

    def as_arrived(value):
        parts = value.transpose(1, 0, 2)[:, :, None]
        return jnp.sum(jnp.where(meets[None, :, :, None], parts, 0.0), axis=1).reshape(2, length)

    table = rope_table(length, HEAD_DIM)
    firsts = [max(b - back, 0) * block for b in range(tensor)]
    numbers = documents.astype(F32)
    docs = jnp.stack([numbers[first : first + (back + 1) * block] for first in firsts])
    own_docs = jnp.pad(numbers.reshape(tensor, block), ((0, 0), (0, back * block)))
    docs = jnp.stack([docs, own_docs], axis=1)
    gains = jnp.stack([query_gain, key_gain])

    def row_of(groups):
        return jnp.concatenate(moves.whole(groups), axis=0)

    def joined(group):
        return jnp.concatenate(group, axis=0)

    weight_qkv = jnp.concatenate([query_weight, key_weight, value_weight], axis=1)
    weight_gate_up = jnp.concatenate([gate_weight, up_weight], axis=1)
    paired = rows == 4 and tensor == 8

    def halves_of(whole):
        return jnp.split(whole, 2)

    def raw_of(*groups):
        return [times(joined(group), weight_qkv) for group in groups]

    hidden_groups, _, raw = moves.gather(hidden_in, early=raw_of)
    raw = raw + raw_of(hidden_groups[-1])
    squares = jnp.stack(
        [
            row_of([jnp.sum(jnp.square(part[:, at : at + local]), axis=1) for part in raw])
            for at in (0, local)
        ]
    )
    raws, raw = raw, row_of(raw)
    sums = moves.add(in_row(squares))
    tables = (sums, gains, table, docs)
    attended_blocks, query, key, value, logsum = attend(shape, order, raws, *tables)
    attended = attended_blocks.reshape(length, local)
    def join_hidden(passing):
        groups, _ = lax.optimization_barrier((hidden_groups, passing))
        return joined_rows(moves.whole(groups))

    attn_proj, _, hidden_all = moves.scatter(
        halves_of(attended),
        lambda part: times(part, output_weight),
        late=join_hidden if tensor == 8 else None,
    )
    if tensor != 8:
        hidden_all = hidden_groups[0][0]
    attn_scale = lax.rsqrt(jnp.mean(attn_proj * attn_proj, axis=1, keepdims=True) + norm_eps)
    attn_unit = attn_proj * attn_scale
    middle = hidden_in.astype(F32) + attn_unit * attention_gain
    middle_low = middle.astype(BF16)

    def activate(both):
        gate, up = both[:, :hidden_units], both[:, hidden_units:]
        return (gate * jax.nn.sigmoid(gate) * up).astype(BF16)

    def both_of(*groups):
        both = [times(joined(group), weight_gate_up) for group in groups]
        return both, [activate(part) for part in both]

    def to_pair(value):
        return lax.ppermute(value, "dp", in_pairs(2))

    def gather_pair(value):
        return lax.all_gather(value, "tensor", axis=0, tiled=True)

    pair_middle = to_pair(middle_low) if paired else None

    def both_early(*groups):
        return both_of(*groups), pair_middle

    middle_groups, _, made = moves.gather(middle_low, early=both_early)
    made, pair_middle = made or (([], []), None)
    if paired:
        pair_middle_all = gather_pair(pair_middle)
    both_groups, activated = (early + late for early, late in zip(made, both_of(middle_groups[-1])))
    activated = lax.optimization_barrier(row_of(activated))
    mlp_proj, _, _ = moves.scatter(halves_of(activated), lambda part: times(part, down_weight))
    mlp_scale = lax.rsqrt(jnp.mean(mlp_proj * mlp_proj, axis=1, keepdims=True) + norm_eps)
    mlp_unit = mlp_proj * mlp_scale
    result = middle + mlp_unit * feedforward_gain

    grad_out = out_grad.astype(F32)
    grad_mlp = norm_back(grad_out, mlp_unit, mlp_scale, feedforward_gain).astype(BF16)
    feedforward_part = jnp.sum(grad_out * mlp_unit, axis=0)
    pair_both = None
    if paired:
        pair_middle_all, grad_mlp = lax.optimization_barrier((pair_middle_all, grad_mlp))
        pair_both = times(pair_middle_all, weight_gate_up).astype(BF16)

    def back_early(near, beside):
        part = feed_back(near, down_weight, both_groups[0], 2, 1)
        part = feed_back(beside, down_weight, both_groups[1], 0, 2, part)
        return part, pair_grad_mlp[1]

    pair_grad_mlp = [None, None]
    if paired:
        first_half, second_half = jnp.split(grad_mlp, 2, axis=1)
        first_half, second_half = lax.optimization_barrier((to_pair(first_half), second_half))
        pair_grad_mlp = [first_half, to_pair(second_half)]
    meanwhile = (pair_both, pair_grad_mlp[0])
    grad_mlp_groups, (pair_both, first_half), made = moves.gather(grad_mlp, meanwhile, back_early)
    if tensor == 8:
        made, second_half = made
        grad_gate_up = feed_back(grad_mlp_groups[-1], down_weight, both_groups[2], 3, 1, made, limit=60)
        grad_gate_up = [half.reshape(length // 2, 2 * hidden_units) for half in grad_gate_up]
    else:
        grad_act = times_transposed(grad_mlp_groups[0][0], down_weight)
        both = both_groups[0].astype(F32)
        grad_gate_up = gated_grad(grad_act, both[:, :hidden_units], both[:, hidden_units:])
        grad_gate_up = halves_of(jnp.concatenate(grad_gate_up, axis=1))
    if paired:
        pair_grad_mlp_all = gather_pair(jnp.concatenate([first_half, second_half], axis=1))

    me = lax.axis_index("dp")
    half_rows = length // 2

    def own_weight_pieces(place):
        blocks = moves.whole(middle_groups) + moves.whole(grad_mlp_groups)
        part = [(at, 0, block) for at in range(16)]
        mine, others, grads = pieces_of(blocks, [part[:4], part[4:8], part[8:]], place)
        return [
            contract_rows(grads, activated),
            contract_rows(mine, grad_gate_up[0]) + contract_rows(others, grad_gate_up[1]),
        ]

    def pair_weight_pieces(place):
        plan = [[(0, 0, half_rows)], [(0, half_rows, half_rows)], [(1, 0, length)]]
        first, second, grads = pieces_of([pair_middle_all, pair_grad_mlp_all], plan, place)
        return [
            contract_rows(grads, pair_activated),
            contract_rows(first, pair_gate_up[0]) + contract_rows(second, pair_gate_up[1]),
        ]

    def gate_up_own(place):
        part = [(at, 0, block) for at in range(8)]
        mine, others = pieces_of(moves.whole(middle_groups), [part[:4], part[4:]], place)
        return contract_rows(mine, grad_gate_up[0]) + contract_rows(others, grad_gate_up[1])

    def gate_up_pair(place):
        plan = [[(0, 0, half_rows)], [(0, half_rows, half_rows)]]
        first, second = pieces_of([pair_middle_all], plan, place)
        return contract_rows(first, pair_gate_up[0]) + contract_rows(second, pair_gate_up[1])

    def down_pieces(place):
        part = [(at, 0, block) for at in range(8)]
        blocks = moves.whole(grad_mlp_groups) + [pair_grad_mlp_all]
        own, pair = pieces_of(blocks, [part, [(8, 0, length)]], place)
        return contract_rows(own, activated) + contract_rows(pair, pair_activated)

    def own_away(sent):
        nonlocal grad_mlp_groups, middle_groups
        grad_mlp_groups, middle_groups, _ = lax.optimization_barrier((grad_mlp_groups, middle_groups, sent))
        return own_weight_pieces(me ^ 1)

    def pair_back(passing):
        grads, _ = lax.optimization_barrier((pair_grad_mlp_all, passing))
        pair_activated, *pair_gate_up = feed_back([grads], down_weight, pair_both, 0, 4, with_activated=True)
        return pair_activated, [half.reshape(half_rows, 2 * hidden_units) for half in pair_gate_up]

    back_part, away, pair_gate_up = moves.scatter(
        grad_gate_up,
        lambda part: times_transposed(part, weight_gate_up),
        own_away if paired else None,
        pair_back if paired else None,
    )
    grad_middle = grad_out + back_part

    grad_proj = norm_back(grad_middle, attn_unit, attn_scale, attention_gain).astype(BF16)
    attention_part = jnp.sum(grad_middle * attn_unit, axis=0)
    if paired:
        (pair_activated, pair_gate_up), grad_proj = lax.optimization_barrier((pair_gate_up, grad_proj))
        away = [(own + pair).astype(BF16) for own, pair in zip(away, pair_weight_pieces(me ^ 1))]
        away = [away[0], *jnp.split(away[1], 2, axis=1)]
        away = [half for part in away for half in jnp.split(part, 2)]
        got = [lax.ppermute(part, "dp", in_pairs(1)) for part in away]

    def attended_early(*groups):
        return [times_transposed(joined(group), output_weight).astype(BF16) for group in groups]

    def proj_early(*groups):
        if not paired:
            return attended_early(*groups), None
        return attended_early(*groups), gate_up_own(me)

    grad_proj_groups, away, made = moves.gather(grad_proj, away, proj_early)
    made, *rest = made or ([],)
    if paired:
        (kept_gate_up,) = rest
    else:
        down_grad = scatter_rows(contract_rows(activated, row_of(grad_mlp_groups)).astype(BF16), 1).astype(F32)
        back = contract_rows(row_of(middle_groups), jnp.concatenate(grad_gate_up, axis=0))
        gate_grad, up_grad = jnp.split(scatter_rows(back.astype(BF16), 0).astype(F32), 2, axis=1)
    grad_attended = made + attended_early(grad_proj_groups[-1])
    raw_blocks = raw.reshape(tensor, block, 3 * local)
    inner, grad_value, products, gain_parts = attend_back(
        shape, order, raw_blocks, *tables, query, key, value, logsum, grad_attended
    )
    if paired:
        (products, grad_proj_groups), *got[:2] = lax.optimization_barrier(
            ((products, grad_proj_groups), *got[:2])
        )
    output_part = sum(
        contract_rows(joined(right), left) for left, right in zip(moves.groups(attended), grad_proj_groups)
    )
    place = lax.axis_index("tensor") * local
    spread = lax.dynamic_update_slice(jnp.zeros((2, width), F32), gain_parts, (0, place))
    spread = jnp.concatenate([spread, attention_part[None], feedforward_part[None]], axis=0)
    packed = moves.add(jnp.concatenate([products.reshape(-1), spread.reshape(-1)]).reshape(-1, 256))
    if paired:
        packed, got[2] = lax.optimization_barrier((packed, got[2]))
    packed = packed.reshape(-1)
    products = as_arrived(packed[: 2 * length].reshape(tensor, 2, block)).T * (1.0 / width)
    gain_sums = add_rows(packed[2 * length :], rows)
    inner = inner.reshape(length, 2 * local)
    grad_qkv = [None, None, grad_value.reshape(length, local)]
    flat = as_arrived(sums).T
    for which in range(2):
        own = slice(which * local, (which + 1) * local)
        inverse = lax.rsqrt(flat[:, which : which + 1] * (1.0 / width) + norm_eps)
        unit = raw[:, own] * inverse
        grad_qkv[which] = (inverse * (inner[:, own] - unit * products[:, which : which + 1])).astype(BF16)
    grad_qkv = jnp.concatenate(grad_qkv, axis=1)
    qkv_part = contract_rows(hidden_all, grad_qkv).astype(BF16)
    projections_part = jnp.concatenate([qkv_part, output_part.astype(BF16)], axis=1)
    if paired:
        projections_part, *got[3:5] = lax.optimization_barrier((projections_part, *got[3:5]))
    grad_qkv, projections_part = lax.optimization_barrier((grad_qkv, projections_part))
    projections_grad = scatter_rows(projections_part, 0)

    def finish_gate(sent):
        nonlocal pair_middle_all, pair_gate_up
        values, _ = lax.optimization_barrier(((pair_middle_all, pair_gate_up), sent))
        pair_middle_all, pair_gate_up = values
        kept = kept_gate_up + gate_up_pair(me)
        gate_got = jnp.concatenate(got[2:4], axis=0).astype(F32)
        return kept[:, :hidden_units] + gate_got, kept[:, hidden_units:]

    def finish_down(passing):
        nonlocal grad_mlp_groups, pair_grad_mlp_all
        values, _ = lax.optimization_barrier(((grad_mlp_groups, pair_grad_mlp_all), passing))
        grad_mlp_groups, pair_grad_mlp_all = values
        return (down_pieces(me) + jnp.concatenate(got[:2], axis=0).astype(F32)).T

    input_part, made, down_made = moves.scatter(
        halves_of(grad_qkv),
        lambda part: times_transposed(part, weight_qkv),
        finish_gate if paired else None,
        finish_down if paired else None,
    )
    input_grad = grad_middle + input_part
    if paired:
        (gate_grad, up_kept), down_grad = made, down_made
        up_grad = up_kept + jnp.concatenate(got[4:], axis=0).astype(F32)
        results = input_grad, down_grad, gate_grad, up_grad
        gain_sums, results = lax.optimization_barrier((gain_sums, results))
        input_grad, down_grad, gate_grad, up_grad = results
        own, one, two, three = gain_sums
        gain_sums = (own + one) + (two + three)
    query_grad, key_grad, value_grad, output_grad = (
        projections_grad[:, at * local : (at + 1) * local].astype(F32) for at in range(4)
    )
    output_grad = output_grad.T
    summed = gain_sums.reshape(4, width)
    return (
        result,
        input_grad,
        query_grad,
        key_grad,
        value_grad,
        output_grad,
        gate_grad,
        up_grad,
        down_grad,
        summed[0],
        summed[1],
        summed[2],
        summed[3],
    )


def solution(mesh):
    in_specs = (
        P(("dp", "tensor"), None),
        P("dp", None),
        P(None, "tensor"),
        P(None, "tensor"),
        P(None, "tensor"),
        P("tensor", None),
        P(None, "tensor"),
        P(None, "tensor"),
        P("tensor", None),
        P("tensor"),
        P("tensor"),
        P(),
        P(),
        P(("dp", "tensor"), None),
    )
    out_specs = (
        P(("dp", "tensor"), None),
        P(("dp", "tensor"), None),
        P("dp", "tensor"),
        P("dp", "tensor"),
        P("dp", "tensor"),
        P("tensor", "dp"),
        P("dp", "tensor"),
        P("dp", "tensor"),
        P("tensor", "dp"),
        P(),
        P(),
        P(),
        P(),
    )
    sizes = {axis: mesh.shape[axis] for axis in ("dp", "tensor")}
    return jax.shard_map(
        functools.partial(body, sizes), mesh=mesh, in_specs=in_specs, out_specs=out_specs, check_vma=False
    )
```
